128 devices in a mesh: row: 8 (over y_lo, x), col: 16 (over z, y_hi, core).
Axes of the slice: x: 4, y: 4 (y_hi: 2, y_lo: 2; y = y_hi * 2 + y_lo), z: 4, core: 2. Of those that a mesh axis runs over, the one named last changes fastest.
Arguments:
- tokens: bfloat16 [2048, 28672], P('row', 'col'), may hold values from -6 to 6
- edit_src: int32 [512, 4], replicated, may hold values from 0 to 2047
- cov_tiles: float32 [8, 16, 1792, 1792], P('row', 'col'), as said below
- cov_far: float32 [16, 896, 1792], P('col', 'row'), may hold values from -0.03125 to 0.03125
- residual: bfloat16 [8192, 512], P('row'), may hold values from -0.25 to 0.25
Outputs:
- delta: bfloat16 [8192, 28672], P('row', 'col')
The draws below stay inside these ranges and needn't reach their ends.
Inputs may be any that keep to these rules, and one draw needn't show every extreme that they name: cov_tiles[0, b] is symmetric for every b.
All inputs are finite; a program needn't handle non-finite values.
Results may differ from the reference program's by a relative error of at most 0.024.
Values may be sent and summed in bfloat16 or wider, within the bound.
A program may use at most 128 MiB of HBM per device.

```python
import jax
import jax.numpy as jnp
from jax import lax

W = 28672
DOUT = 8192
NK = 512
CTX = 4
TOKENS = 2048
BLOCKS = 16
TILE = 1792
N_ROW = 8
N_COL = 16


def draw_cov_tiles(key, part):
    key_base, key_lead = jax.random.split(key, 2)
    tile_shape = (N_ROW, N_COL, TILE, TILE)
    base_draw = jax.random.normal(key_base, tile_shape, jnp.float32)
    base_draw = base_draw * W ** (-0.5)
    symmetric = (base_draw[0] + jnp.swapaxes(base_draw[0], 1, 2)) * 0.70710678
    lead_diag = jax.random.uniform(key_lead, (N_COL, TILE), jnp.float32, 0.5, 2.0)
    identity = jnp.eye(TILE, dtype=jnp.float32)
    diag_tiles = symmetric + lead_diag[:, :, None] * identity[None, :, :]
    return base_draw.at[0].set(diag_tiles)


def set_ends(result, own_key, least, top_value):
    longest = result.shape.index(max(result.shape))
    spots = []
    for shift in (0, 1):
        where = [jax.random.randint(jax.random.fold_in(own_key, axis), (), 0, length) for axis, length in enumerate(result.shape)]
        where[longest] = (where[longest] + shift) % result.shape[longest]
        spots.append(tuple(where))
    return result.at[spots[0]].set(least).at[spots[1]].set(top_value)


def block_scale(own_key, extent, shards, low, largest):
    def one(axis_at, parts):
        heights = jax.random.uniform(jax.random.fold_in(jax.random.fold_in(own_key, 6), axis_at), (parts,), jnp.float32, low / len(shards), largest / len(shards))
        return jnp.repeat(jnp.exp(heights), extent[axis_at] // parts).reshape((-1,) + (1,) * (len(extent) - axis_at - 1))

    loudness = one(*shards[0])
    for cut in shards[1:]:
        loudness = loudness * one(*cut)
    return loudness


def centred(key, extent, width, limit, shards=(), held_as=jnp.bfloat16):
    array = width * jax.random.normal(key, extent, jnp.float32)
    if shards:
        array = array * block_scale(key, extent, shards, -0.22, 0.18)
    return jnp.clip(array, -limit, limit).astype(held_as)


def setup_inputs(seed: int = 0) -> dict:
    splits = jax.random.split(jax.random.key(seed), 6)
    return {
        "tokens": centred(splits[0], (TOKENS, W), 1.0, 6.0, ((0, 8), (1, 16))),
        "edit_src": set_ends(jax.random.randint(splits[1], (NK, CTX), 0, TOKENS), jax.random.fold_in(splits[1], 1), 0, TOKENS - 1).astype(jnp.int32),
        "cov_tiles": draw_cov_tiles(jax.random.fold_in(splits[5], 71), 0),
        "cov_far": centred(splits[3], (BLOCKS, TILE // 2, TILE), W ** -0.5, 0.03125, ((0, 16), (1, 8)), jnp.float32),
        "residual": centred(splits[4], (DOUT, NK), NK ** -0.5, 0.25, ((0, 8),)),
    }


def reference(tokens, edit_src, cov_tiles, cov_far, residual):
    tile_width = W // N_COL
    half_width = tile_width // 2
    highest = lax.Precision.HIGHEST
    gathered = jnp.take(tokens, edit_src, axis=0)
    keys = (jnp.sum(gathered.astype(jnp.float32), axis=1) / CTX).astype(jnp.bfloat16)
    keys_float = keys.astype(jnp.float32)
    summed = jnp.zeros((NK, W), jnp.float32)
    for lag_index in range(N_ROW):
        for col_high in range(N_COL):
            col_low = (col_high - lag_index) % N_COL
            cov_block = cov_tiles[lag_index, col_high]
            low_keys = keys_float[:, col_low * tile_width:(col_low + 1) * tile_width]
            summed = summed.at[:, col_high * tile_width:(col_high + 1) * tile_width].add(
                jnp.dot(low_keys, cov_block, precision=highest, preferred_element_type=jnp.float32))
            if lag_index > 0:
                high_keys = keys_float[:, col_high * tile_width:(col_high + 1) * tile_width]
                summed = summed.at[:, col_low * tile_width:(col_low + 1) * tile_width].add(
                    jnp.dot(high_keys, cov_block.T, precision=highest, preferred_element_type=jnp.float32))
    for far_index in range(N_COL):
        col_low = far_index % N_ROW
        col_high = col_low + N_ROW
        row_start = col_low * tile_width + (far_index // N_ROW) * half_width
        far_slab = cov_far[far_index]
        summed = summed.at[:, col_high * tile_width:(col_high + 1) * tile_width].add(
            jnp.dot(keys_float[:, row_start:row_start + half_width], far_slab, precision=highest, preferred_element_type=jnp.float32))
        summed = summed.at[:, row_start:row_start + half_width].add(
            jnp.dot(keys_float[:, col_high * tile_width:(col_high + 1) * tile_width], far_slab.T, precision=highest, preferred_element_type=jnp.float32))
    q_matrix = summed.astype(jnp.bfloat16)
    return jnp.dot(residual, q_matrix, preferred_element_type=jnp.float32).astype(jnp.bfloat16)
```

```python
import functools

import jax
import jax.numpy as jnp
from jax import lax
from jax.experimental import pallas as pl
from jax.experimental.pallas import tpu as pltpu
from jax.sharding import PartitionSpec as P

MESH = pl.DeviceIdType.MESH
F32 = jnp.float32
BF16 = jnp.bfloat16
NX = 4
NROW = 8
NCOL = 16
SLAB = 16


def remote(src, dst, send_sem, recv_sem, row, col):
    return pltpu.make_async_remote_copy(
        src_ref=src,
        dst_ref=dst,
        send_sem=send_sem,
        recv_sem=recv_sem,
        device_id=(row, col),
        device_id_type=MESH,
    )


def add_rows(out_ref, out_at, rows, terms):
    def step(i, carry):
        at = pl.multiple_of(i * SLAB, SLAB)
        total = None
        for ref, start in terms:
            part = ref[pl.ds(pl.multiple_of(start + at, SLAB), SLAB), :].astype(F32)
            total = part if total is None else total + part
        out_ref[pl.ds(pl.multiple_of(out_at + at, SLAB), SLAB), :] = total.astype(out_ref.dtype)
        return carry

    lax.fori_loop(0, rows // SLAB, step, 0)


def kernel(
    edit_ref, tok_ref, cov_ref, far_ref, out_ref,
    counts, part, cov_f, cov, slab_f, slab_send, slab_in, slab_pad,
    own, lag, mir, direct, win, nout_send, nout,
    k_ra1, k_ra2, k_rb1, k_rb2, k_sa, k_sb,
    q_ra1, q_ra2, q_rb1, q_rb2, q_sa, q_sb, m_in, q_sum, q_all,
    cov_sem, slab_sem, loc_sem,
    krs_s, krs_r, kag_s, kag_r, qrs_s, qrs_r, qag_s, qag_r,
    lag_s, lag_r, mir_s, mir_r, far_s, far_r,
):
    r = lax.axis_index("row")
    c = lax.axis_index("col")
    x = r % NX
    yl = r // NX
    ry = (r + NX) % NROW
    edits, width = own.shape
    half = edits // 2
    ch = half // NROW
    tok_dev = tok_ref.shape[0]
    tile = 256
    tiles = width // tile
    far_rows = slab_f.shape[0]

    def across(d):
        return yl * NX + (x + d) % NX

    def lag_col(i):
        return (c + i) % NCOL

    base_col = (c + NCOL - r) % NCOL
    low = c < NCOL // 2
    far_col = (c + NCOL // 2) % NCOL

    def chunk_a(row):
        return pl.multiple_of((row % NX) * (2 * ch) + (row // NX) * ch, ch)

    def chunk_b(row):
        return pl.multiple_of(half + (row // NX) * (NX * ch) + (row % NX) * ch, ch)

    def cov_copy(i):
        rows = pl.ds(i * tile, tile)
        return pltpu.make_async_copy(cov_ref.at[0, 0, rows], cov_f.at[rows], cov_sem.at[i])

    slab_copy = pltpu.make_async_copy(far_ref.at[0], slab_f, slab_sem)
    barrier = pltpu.get_barrier_semaphore()

    def greet(row, col):
        pl.semaphore_signal(barrier, inc=1, device_id=(row, col), device_id_type=MESH)

    for d in range(1, NX):
        greet(across(d), c)
    greet(ry, c)
    greet(r, far_col)

    def greet_lag(i, carry):
        greet(i, lag_col(i))
        return carry

    lax.fori_loop(1, NROW, greet_lag, 0)

    def greet_base(i, carry):
        greet(i, base_col)
        return carry

    @pl.when(r > 0)
    def _():
        lax.fori_loop(0, NROW, greet_base, 0)

    slab_copy.start()
    for i in range(tiles):
        cov_copy(i).start()

    def count_rows(i, carry):
        rows = pl.ds(pl.multiple_of(i * 64, 64), 64)
        relative = edit_ref[rows, :] - r * tok_dev
        slots = lax.broadcasted_iota(jnp.int32, (64, tok_dev), 1)
        total = jnp.zeros((64, tok_dev), F32)
        for j in range(edit_ref.shape[1]):
            total = total + (relative[:, j : j + 1] == slots).astype(F32)
        counts[rows, :] = (total / edit_ref.shape[1]).astype(BF16)
        return carry

    lax.fori_loop(0, edits // 64, count_rows, 0)

    def partial_keys(h):
        def step(n, carry):
            columns = pl.ds(pl.multiple_of(n * tile, tile), tile)
            part[pl.ds(h * half, half), columns] = jnp.dot(
                counts[pl.ds(h * half, half), :], tok_ref[:, columns], preferred_element_type=F32
            ).astype(BF16)
            return carry

        lax.fori_loop(0, tiles, step, 0)

    def rs_a1(src, ra1, ss, rs, d):
        rows = pl.ds(pl.multiple_of(((x + d) % NX) * (2 * ch), 2 * ch), 2 * ch)
        return remote(src.at[rows], ra1.at[d - 1], ss.at[d - 1], rs.at[d - 1], across(d), c)

    def rs_b1(src, rb1, ss, rs):
        rows = pl.ds(pl.multiple_of(half + (1 - yl) * (NX * ch), NX * ch), NX * ch)
        return remote(src.at[rows], rb1, ss.at[3], rs.at[3], ry, c)

    def rs_a2(sa, ra2, ss, rs):
        rows = pl.ds(pl.multiple_of((1 - yl) * ch, ch), ch)
        return remote(sa.at[rows], ra2, ss.at[4], rs.at[4], ry, c)

    def rs_b2(sb, rb2, ss, rs, d):
        rows = pl.ds(pl.multiple_of(((x + d) % NX) * ch, ch), ch)
        return remote(sb.at[rows], rb2.at[d - 1], ss.at[4 + d], rs.at[4 + d], across(d), c)

    def rs_middle(src, ra1, ra2, rb1, rb2, sa, sb, ss, rs):
        rs_b1(src, rb1, ss, rs).wait_recv()
        add_rows(sb, 0, NX * ch, [(src, half + yl * (NX * ch)), (rb1, 0)])
        for d in range(1, NX):
            rs_b2(sb, rb2, ss, rs, d).start()
        for d in range(1, NX):
            rs_a1(src, ra1, ss, rs, d).wait_recv()
        add_rows(sa, 0, 2 * ch, [(src, x * (2 * ch))] + [(ra1.at[d], 0) for d in range(NX - 1)])
        rs_a2(sa, ra2, ss, rs).start()

    def rs_end(ra2, rb2, sa, sb, ss, rs, out, a_more, b_more):
        rs_a2(sa, ra2, ss, rs).wait_recv()
        add_rows(out, chunk_a(r), ch, [(sa, yl * ch), (ra2, 0)] + a_more)
        for d in range(1, NX):
            rs_b2(sb, rb2, ss, rs, d).wait_recv()
        add_rows(out, chunk_b(r), ch, [(sb, x * ch)] + [(rb2.at[d], 0) for d in range(NX - 1)] + b_more)

    def rs_sent(src, ra1, ra2, rb1, rb2, sa, sb, ss, rs):
        rs_b1(src, rb1, ss, rs).wait_send()
        rs_a2(sa, ra2, ss, rs).wait_send()
        for d in range(1, NX):
            rs_a1(src, ra1, ss, rs, d).wait_send()
            rs_b2(sb, rb2, ss, rs, d).wait_send()

    def ag_a1(full, ss, rs, row):
        rows = pl.ds(chunk_a(row), ch)
        return remote(full.at[rows], full.at[rows], ss.at[0], rs.at[0], ry, c)

    def ag_b1(full, ss, rs, row, d):
        rows = pl.ds(chunk_b(row), ch)
        return remote(full.at[rows], full.at[rows], ss.at[d], rs.at[d], across(d), c)

    def ag_a2(full, ss, rs, xx, d):
        rows = pl.ds(pl.multiple_of(xx * (2 * ch), 2 * ch), 2 * ch)
        return remote(full.at[rows], full.at[rows], ss.at[3 + d], rs.at[3 + d], across(d), c)

    def ag_b2(full, ss, rs, yy):
        rows = pl.ds(pl.multiple_of(half + yy * (NX * ch), NX * ch), NX * ch)
        return remote(full.at[rows], full.at[rows], ss.at[7], rs.at[7], ry, c)

    def ag_start(full, ss, rs):
        ag_a1(full, ss, rs, r).start()
        for d in range(1, NX):
            ag_b1(full, ss, rs, r, d).start()

    def behind(d):
        return (x + NX - d) % NX

    def ag_middle(full, ss, rs):
        ag_a1(full, ss, rs, ry).wait_recv()
        for d in range(1, NX):
            ag_a2(full, ss, rs, x, d).start()
        for d in range(1, NX):
            ag_b1(full, ss, rs, yl * NX + behind(d), d).wait_recv()
        ag_b2(full, ss, rs, yl).start()

    def ag_end(full, ss, rs):
        for d in range(1, NX):
            ag_a2(full, ss, rs, behind(d), d).wait_recv()
        ag_b2(full, ss, rs, 1 - yl).wait_recv()

    def ag_sent(full, ss, rs):
        ag_a1(full, ss, rs, r).wait_send()
        for d in range(1, NX):
            ag_b1(full, ss, rs, r, d).wait_send()
            ag_a2(full, ss, rs, x, d).wait_send()
        ag_b2(full, ss, rs, yl).wait_send()

    def lag_copy(h, source, i):
        rows = pl.ds((chunk_a if h == 0 else chunk_b)(source), ch)
        return remote(
            own.at[rows], lag.at[rows], lag_s.at[i, h], lag_r.at[source, h], i, lag_col(i)
        )

    def mir_copy(h, e, slot):
        rows = pl.ds((chunk_a if h == 0 else chunk_b)(e), ch)
        return remote(
            mir.at[rows], m_in.at[slot, h], mir_s.at[e, h], mir_r.at[slot, h], e, base_col
        )

    def each(low_end, high_end, do):
        def step(i, carry):
            do(i)
            return carry

        lax.fori_loop(low_end, high_end, step, 0)

    at_0 = r * far_rows
    at_1 = width // 2 + r * far_rows
    start_0 = pl.multiple_of(at_0 // 128 * 128, 128)
    start_1 = pl.multiple_of(jnp.minimum(at_1 // 128 * 128, width - tile), 128)

    def slab_far():
        return remote(slab_send, slab_in, far_s.at[0], far_r.at[0], r, far_col)

    def win_far(h):
        columns = pl.ds(start_0 if h == 0 else start_1, tile)
        return remote(
            own.at[:, columns], win.at[:, pl.ds(h * tile, tile)], far_s.at[1 + h], far_r.at[1 + h], r, far_col
        )

    def nout_far():
        return remote(nout_send, nout, far_s.at[3], far_r.at[3], r, far_col)

    krs = (part, k_ra1, k_ra2, k_rb1, k_rb2, k_sa, k_sb, krs_s, krs_r)
    qrs = (direct, q_ra1, q_ra2, q_rb1, q_rb2, q_sa, q_sb, qrs_s, qrs_r)

    partial_keys(0)
    pl.semaphore_wait(barrier, 5 + NROW - 1 + jnp.where(r > 0, NROW, 0))
    for d in range(1, NX):
        rs_a1(part, k_ra1, krs_s, krs_r, d).start()
    partial_keys(1)
    rs_b1(part, k_rb1, krs_s, krs_r).start()

    slab_copy.wait()

    @pl.when(low)
    def _():
        add_rows(slab_send, 0, far_rows, [(slab_f, 0)])
        slab_far().start()

    for i in range(tiles):
        cov_copy(i).wait()
        add_rows(cov, i * tile, tile, [(cov_f, i * tile)])

    @pl.when(jnp.logical_not(low))
    def _():
        slab_pad[...] = jnp.zeros_like(slab_pad)
        add_rows(slab_pad, tile + at_1 - start_1, far_rows, [(slab_f, 0)])

    rs_middle(*krs)
    rs_end(k_ra2, k_rb2, k_sa, k_sb, krs_s, krs_r, own, [], [])
    ag_start(own, kag_s, kag_r)
    ag_middle(own, kag_s, kag_r)

    def send_lag(i):
        lag_copy(0, r, i).start()
        lag_copy(1, r, i).start()

    each(1, NROW, send_lag)

    @pl.when(jnp.logical_not(low))
    def _():
        slab_far().wait_recv()
        add_rows(slab_pad, at_0 - start_0, far_rows, [(slab_in, 0)])

    ag_end(own, kag_s, kag_r)

    @pl.when(low)
    def _():
        win_far(0).start()
        win_far(1).start()

    contract_last = (((1,), (1,)), ((), ()))

    @pl.when(r > 0)
    def _():
        def mirror(n):
            block = pl.ds(pl.multiple_of(n * tile, tile), tile)
            mir[:, block] = lax.dot_general(
                own[...], cov[block, :], contract_last, preferred_element_type=F32
            ).astype(BF16)

        each(0, tiles, mirror)

        def send_mir(e):
            mir_copy(0, e, r - 1).start()
            mir_copy(1, e, r - 1).start()

        each(0, NROW, send_mir)

    @pl.when(jnp.logical_not(low))
    def _():
        def narrow(n):
            block = pl.ds(pl.multiple_of(n * tile, tile), tile)
            nout_send[:, block] = lax.dot_general(
                own[...], slab_pad[block, :], contract_last, preferred_element_type=F32
            ).astype(BF16)

        each(0, 2, narrow)
        nout_far().start()

    own_to_lag = pltpu.make_async_copy(own, lag, loc_sem)

    @pl.when(r == 0)
    def _():
        own_to_lag.start()
        own_to_lag.wait()

    @pl.when(r > 0)
    def _():
        def got_lag(e):
            lag_copy(0, e, 0).wait_recv()
            lag_copy(1, e, 0).wait_recv()

        each(0, NROW, got_lag)

    @pl.when(low)
    def _():
        def step(n):
            block = pl.ds(pl.multiple_of(n * tile, tile), tile)
            direct[:, block] = jnp.dot(
                lag[...], cov[:, block], preferred_element_type=F32
            ).astype(BF16)

        each(0, tiles, step)
        nout_far().wait_recv()

        def add_narrow(i):
            rows = pl.ds(pl.multiple_of(i * 64, 64), 64)
            for h, start in ((0, start_0), (1, start_1)):
                columns = pl.ds(start, tile)
                direct[rows, columns] = (
                    direct[rows, columns].astype(F32)
                    + nout[rows, pl.ds(h * tile, tile)].astype(F32)
                ).astype(BF16)

        each(0, edits // 64, add_narrow)

    @pl.when(jnp.logical_not(low))
    def _():
        win_far(0).wait_recv()
        win_far(1).wait_recv()

        def step(n):
            block = pl.ds(pl.multiple_of(n * tile, tile), tile)
            direct[:, block] = (
                jnp.dot(lag[...], cov[:, block], preferred_element_type=F32)
                + jnp.dot(win[...], slab_pad[:, block], preferred_element_type=F32)
            ).astype(BF16)

        each(0, tiles, step)

    for d in range(1, NX):
        rs_a1(direct, q_ra1, qrs_s, qrs_r, d).start()
    rs_b1(direct, q_rb1, qrs_s, qrs_r).start()
    rs_middle(*qrs)

    def got_mir(i):
        mir_copy(0, r, i).wait_recv()
        mir_copy(1, r, i).wait_recv()

    each(0, NROW - 1, got_mir)
    for h in range(2):
        add_rows(q_sum, h * ch, ch, [(m_in.at[i, h], 0) for i in range(NROW - 1)])
    rs_end(q_ra2, q_rb2, q_sa, q_sb, qrs_s, qrs_r, q_all, [(q_sum, 0)], [(q_sum, ch)])
    ag_start(q_all, qag_s, qag_r)
    ag_middle(q_all, qag_s, qag_r)
    ag_end(q_all, qag_s, qag_r)
    result = pltpu.make_async_copy(q_all, out_ref, loc_sem)
    result.start()

    rs_sent(*krs)
    rs_sent(*qrs)
    ag_sent(own, kag_s, kag_r)
    ag_sent(q_all, qag_s, qag_r)

    def lag_sent(i):
        lag_copy(0, r, i).wait_send()
        lag_copy(1, r, i).wait_send()

    each(1, NROW, lag_sent)

    @pl.when(r > 0)
    def _():
        def mir_sent(e):
            mir_copy(0, e, r - 1).wait_send()
            mir_copy(1, e, r - 1).wait_send()

        each(0, NROW, mir_sent)

    @pl.when(low)
    def _():
        slab_far().wait_send()
        win_far(0).wait_send()
        win_far(1).wait_send()

    @pl.when(jnp.logical_not(low))
    def _():
        nout_far().wait_send()

    result.wait()


def delta_kernel(residual_ref, q_ref, out_ref):
    out_ref[...] = jnp.dot(residual_ref[...], q_ref[...], preferred_element_type=F32).astype(
        out_ref.dtype
    )


def shards(tokens, edit_src, cov_tiles, cov_far, residual):
    edits = edit_src.shape[0]
    tok_dev, width = tokens.shape
    ch = edits // 2 // NROW
    far_rows = cov_far.shape[1]
    tiles = width // 256

    def buf(*shape, dtype=BF16):
        return pltpu.VMEM(shape, dtype)

    def dma(*shape):
        return pltpu.SemaphoreType.DMA(shape)

    def reduce_bufs():
        return [
            buf(NX - 1, 2 * ch, width), buf(ch, width), buf(NX * ch, width),
            buf(NX - 1, ch, width), buf(2 * ch, width), buf(NX * ch, width),
        ]

    q_block = pl.pallas_call(
        kernel,
        name="edit_product",
        out_shape=jax.ShapeDtypeStruct((edits, width), BF16),
        in_specs=[
            pl.BlockSpec(memory_space=pltpu.VMEM),
            pl.BlockSpec(memory_space=pltpu.VMEM),
            pl.BlockSpec(memory_space=pl.ANY),
            pl.BlockSpec(memory_space=pl.ANY),
        ],
        out_specs=pl.BlockSpec(memory_space=pl.ANY),
        scratch_shapes=[
            buf(edits, tok_dev), buf(edits, width),
            buf(width, width, dtype=F32), buf(width, width),
            buf(far_rows, width, dtype=F32), buf(far_rows, width), buf(far_rows, width), buf(512, width),
            buf(edits, width), buf(edits, width), buf(edits, width), buf(edits, width),
            buf(edits, 512), buf(edits, 512), buf(edits, 512),
            *reduce_bufs(),
            *reduce_bufs(),
            buf(NROW - 1, 2, ch, width), buf(2 * ch, width, dtype=F32), buf(edits, width),
            dma(tiles), pltpu.SemaphoreType.DMA, pltpu.SemaphoreType.DMA,
            dma(8), dma(8), dma(8), dma(8), dma(8), dma(8), dma(8), dma(8),
            dma(NROW, 2), dma(NROW, 2), dma(NROW, 2), dma(NROW - 1, 2), dma(4), dma(4),
        ],
        compiler_params=pltpu.CompilerParams(
            collective_id=0, has_side_effects=True, vmem_limit_bytes=60 * 2**20
        ),
    )(edit_src, tokens, cov_tiles, cov_far)

    rows = residual.shape[0]
    step = 256
    return pl.pallas_call(
        delta_kernel,
        name="delta",
        grid=(rows // step,),
        out_shape=jax.ShapeDtypeStruct((rows, width), BF16),
        in_specs=[
            pl.BlockSpec((step, edits), lambda i: (i, 0)),
            pl.BlockSpec((edits, width), lambda i: (0, 0)),
        ],
        out_specs=pl.BlockSpec((step, width), lambda i: (i, 0)),
        compiler_params=pltpu.CompilerParams(vmem_limit_bytes=32 * 2**20),
    )(residual, q_block)


def solution(mesh):
    placed = (
        P("row", "col"),
        P(),
        P("row", "col", None, None),
        P("col", "row", None),
        P("row", None),
    )
    return jax.shard_map(
        shards, mesh=mesh, in_specs=placed, out_specs=P("row", "col"), check_vma=False
    )
```

```python
import functools

import jax
import jax.numpy as jnp
from jax import lax
from jax.experimental import pallas as pl
from jax.experimental.pallas import tpu as pltpu
from jax.sharding import PartitionSpec as P

MESH = pl.DeviceIdType.MESH
F32 = jnp.float32
BF16 = jnp.bfloat16
NX = 4
NROW = 8
NCOL = 16
PLANE = 4
SLAB = 16


def remote(src, dst, send_sem, recv_sem, row, col):
    return pltpu.make_async_remote_copy(
        src_ref=src,
        dst_ref=dst,
        send_sem=send_sem,
        recv_sem=recv_sem,
        device_id=(row, col),
        device_id_type=MESH,
    )


def add_rows(out_ref, out_at, rows, terms):
    def step(i, carry):
        at = pl.multiple_of(i * SLAB, SLAB)
        total = None
        for ref, start in terms:
            part = ref[pl.ds(pl.multiple_of(start + at, SLAB), SLAB), :].astype(F32)
            total = part if total is None else total + part
        out_ref[pl.ds(pl.multiple_of(out_at + at, SLAB), SLAB), :] = total.astype(out_ref.dtype)
        return carry

    lax.fori_loop(0, rows // SLAB, step, 0)


def kernel(
    edit_ref, tok_ref, cov_ref, far_ref, out_ref,
    counts, part, cov_f, cov, slab_f, slab_send, slab_in, slab_pad,
    own, lag, mir, direct, win, nout_send, nout,
    k_ra1, k_ra2, k_rb1, k_rb2, k_sa, k_sb,
    q_ra1, q_ra2, q_rb1, q_rb2, q_sa, q_sb, m_in, q_sum, q_all, relay, crossed, cross_in,
    cov_sem, slab_sem, loc_sem,
    krs_s, krs_r, kag_s, kag_r, qrs_s, qrs_r, qag_s, qag_r,
    lag_s, lag_r, mir_s, mir_r, far_s, far_r, rel_s, rel_r, cross_s, cross_r, stay_sem,
):
    r = lax.axis_index("row")
    c = lax.axis_index("col")
    x = r % NX
    yl = r // NX
    ry = (r + NX) % NROW
    edits, width = own.shape
    half = edits // 2
    ch = half // NROW
    tok_dev = tok_ref.shape[0]
    tile = 256
    tiles = width // tile
    far_rows = slab_f.shape[0]

    def across(d):
        return yl * NX + (x + d) % NX

    u = c % PLANE
    plane = c - u
    is_mid = r == PLANE

    def ahead(i):
        return plane + (u + i) % PLANE

    source_col = plane + (u + NCOL - r) % PLANE
    up_col = (c + PLANE) % NCOL
    down_col = (c + NCOL - PLANE) % NCOL
    low = c < NCOL // 2
    far_col = (c + NCOL // 2) % NCOL

    def chunk_a(row):
        return pl.multiple_of((row % NX) * (2 * ch) + (row // NX) * ch, ch)

    def chunk_b(row):
        return pl.multiple_of(half + (row // NX) * (NX * ch) + (row % NX) * ch, ch)

    def cov_copy(i):
        rows = pl.ds(i * tile, tile)
        return pltpu.make_async_copy(cov_ref.at[0, 0, rows], cov_f.at[rows], cov_sem.at[i])

    slab_copy = pltpu.make_async_copy(far_ref.at[0], slab_f, slab_sem)
    barrier = pltpu.get_barrier_semaphore()

    def greet(row, col):
        pl.semaphore_signal(barrier, inc=1, device_id=(row, col), device_id_type=MESH)

    for d in range(1, NX):
        greet(across(d), c)
    greet(ry, c)
    greet(r, far_col)
    greet(r, up_col)
    greet(r, down_col)

    def each(low_end, high_end, do):
        def step(i, carry):
            do(i)
            return carry

        lax.fori_loop(low_end, high_end, step, 0)

    def others(low_end, high_end, do):
        def step(i):
            @pl.when(jnp.logical_not(jnp.logical_and(is_mid, i == PLANE)))
            def _():
                do(i)

        each(low_end, high_end, step)

    others(1, NROW, lambda i: greet(i, ahead(i)))

    @pl.when(r > 0)
    def _():
        others(0, NROW, lambda e: greet(e, source_col))

    slab_copy.start()
    for i in range(tiles):
        cov_copy(i).start()

    def count_rows(i, carry):
        rows = pl.ds(pl.multiple_of(i * 64, 64), 64)
        relative = edit_ref[rows, :] - r * tok_dev
        slots = lax.broadcasted_iota(jnp.int32, (64, tok_dev), 1)
        total = jnp.zeros((64, tok_dev), F32)
        for j in range(edit_ref.shape[1]):
            total = total + (relative[:, j : j + 1] == slots).astype(F32)
        counts[rows, :] = (total / edit_ref.shape[1]).astype(BF16)
        return carry

    lax.fori_loop(0, edits // 64, count_rows, 0)

    def partial_keys(h):
        def step(n, carry):
            columns = pl.ds(pl.multiple_of(n * tile, tile), tile)
            part[pl.ds(h * half, half), columns] = jnp.dot(
                counts[pl.ds(h * half, half), :], tok_ref[:, columns], preferred_element_type=F32
            ).astype(BF16)
            return carry

        lax.fori_loop(0, tiles, step, 0)

    def rs_a1(src, ra1, ss, rs, d):
        rows = pl.ds(pl.multiple_of(((x + d) % NX) * (2 * ch), 2 * ch), 2 * ch)
        return remote(src.at[rows], ra1.at[d - 1], ss.at[d - 1], rs.at[d - 1], across(d), c)

    def rs_b1(src, rb1, ss, rs):
        rows = pl.ds(pl.multiple_of(half + (1 - yl) * (NX * ch), NX * ch), NX * ch)
        return remote(src.at[rows], rb1, ss.at[3], rs.at[3], ry, c)

    def rs_a2(sa, ra2, ss, rs):
        rows = pl.ds(pl.multiple_of((1 - yl) * ch, ch), ch)
        return remote(sa.at[rows], ra2, ss.at[4], rs.at[4], ry, c)

    def rs_b2(sb, rb2, ss, rs, d):
        rows = pl.ds(pl.multiple_of(((x + d) % NX) * ch, ch), ch)
        return remote(sb.at[rows], rb2.at[d - 1], ss.at[4 + d], rs.at[4 + d], across(d), c)

    def rs_middle(src, ra1, ra2, rb1, rb2, sa, sb, ss, rs):
        rs_b1(src, rb1, ss, rs).wait_recv()
        add_rows(sb, 0, NX * ch, [(src, half + yl * (NX * ch)), (rb1, 0)])
        for d in range(1, NX):
            rs_b2(sb, rb2, ss, rs, d).start()
        for d in range(1, NX):
            rs_a1(src, ra1, ss, rs, d).wait_recv()
        add_rows(sa, 0, 2 * ch, [(src, x * (2 * ch))] + [(ra1.at[d], 0) for d in range(NX - 1)])
        rs_a2(sa, ra2, ss, rs).start()

    def rs_end(ra2, rb2, sa, sb, ss, rs, out, a_more, b_more):
        rs_a2(sa, ra2, ss, rs).wait_recv()
        add_rows(out, chunk_a(r), ch, [(sa, yl * ch), (ra2, 0)] + a_more)
        for d in range(1, NX):
            rs_b2(sb, rb2, ss, rs, d).wait_recv()
        add_rows(out, chunk_b(r), ch, [(sb, x * ch)] + [(rb2.at[d], 0) for d in range(NX - 1)] + b_more)

    def rs_sent(src, ra1, ra2, rb1, rb2, sa, sb, ss, rs):
        rs_b1(src, rb1, ss, rs).wait_send()
        rs_a2(sa, ra2, ss, rs).wait_send()
        for d in range(1, NX):
            rs_a1(src, ra1, ss, rs, d).wait_send()
            rs_b2(sb, rb2, ss, rs, d).wait_send()

    def ag_a1(full, ss, rs, row):
        rows = pl.ds(chunk_a(row), ch)
        return remote(full.at[rows], full.at[rows], ss.at[0], rs.at[0], ry, c)

    def ag_b1(full, ss, rs, row, d):
        rows = pl.ds(chunk_b(row), ch)
        return remote(full.at[rows], full.at[rows], ss.at[d], rs.at[d], across(d), c)

    def ag_a2(full, ss, rs, xx, d):
        rows = pl.ds(pl.multiple_of(xx * (2 * ch), 2 * ch), 2 * ch)
        return remote(full.at[rows], full.at[rows], ss.at[3 + d], rs.at[3 + d], across(d), c)

    def ag_b2(full, ss, rs, yy):
        rows = pl.ds(pl.multiple_of(half + yy * (NX * ch), NX * ch), NX * ch)
        return remote(full.at[rows], full.at[rows], ss.at[7], rs.at[7], ry, c)

    def ag_start(full, ss, rs):
        ag_a1(full, ss, rs, r).start()
        for d in range(1, NX):
            ag_b1(full, ss, rs, r, d).start()

    def behind(d):
        return (x + NX - d) % NX

    def ag_middle(full, ss, rs):
        ag_a1(full, ss, rs, ry).wait_recv()
        for d in range(1, NX):
            ag_a2(full, ss, rs, x, d).start()
        for d in range(1, NX):
            ag_b1(full, ss, rs, yl * NX + behind(d), d).wait_recv()
        ag_b2(full, ss, rs, yl).start()

    def ag_end(full, ss, rs):
        for d in range(1, NX):
            ag_a2(full, ss, rs, behind(d), d).wait_recv()
        ag_b2(full, ss, rs, 1 - yl).wait_recv()

    def ag_sent(full, ss, rs):
        ag_a1(full, ss, rs, r).wait_send()
        for d in range(1, NX):
            ag_b1(full, ss, rs, r, d).wait_send()
            ag_a2(full, ss, rs, x, d).wait_send()
        ag_b2(full, ss, rs, yl).wait_send()

    def chunk(h, row):
        return pl.ds((chunk_a if h == 0 else chunk_b)(row), ch)

    def relay_copy(h, far):
        return remote(
            own.at[chunk(h, r)], relay.at[far, h], rel_s.at[far, h], rel_r.at[far, h], r,
            far_col if far else up_col,
        )

    def lag_copy(h, source, i, held):
        return remote(
            held, lag.at[chunk(h, source)], lag_s.at[i, h], lag_r.at[source, h], i, ahead(i)
        )

    def lag_stay(h, held):
        return pltpu.make_async_copy(held, lag.at[chunk(h, r)], stay_sem.at[h])

    def mir_copy(h, e, slot):
        return remote(
            mir.at[chunk(h, e)], m_in.at[slot, h], mir_s.at[e, h], mir_r.at[slot, h], e, source_col
        )

    def mir_stay(h):
        return pltpu.make_async_copy(mir.at[chunk(h, r)], m_in.at[PLANE - 1, h], stay_sem.at[2 + h])

    def cross_copy(far):
        return remote(
            crossed.at[far], cross_in.at[far], cross_s.at[far], cross_r.at[far], r,
            far_col if far else down_col,
        )

    def add_slots(out, out_at, first, last):
        for h in range(2):
            def step(i, carry):
                rows = pl.ds(pl.multiple_of(i * SLAB, SLAB), SLAB)
                total = lax.fori_loop(
                    first, last,
                    lambda slot, so_far: so_far + m_in[slot, h, rows, :].astype(F32),
                    jnp.zeros((SLAB, width), F32),
                )
                out[pl.ds(pl.multiple_of(out_at + h * ch + i * SLAB, SLAB), SLAB), :] = total.astype(out.dtype)
                return carry

            lax.fori_loop(0, ch // SLAB, step, 0)

    at_0 = r * far_rows
    at_1 = width // 2 + r * far_rows
    start_0 = pl.multiple_of(at_0 // 128 * 128, 128)
    start_1 = pl.multiple_of(jnp.minimum(at_1 // 128 * 128, width - tile), 128)

    def slab_far():
        return remote(slab_send, slab_in, far_s.at[0], far_r.at[0], r, far_col)

    def win_far(h):
        columns = pl.ds(start_0 if h == 0 else start_1, tile)
        return remote(
            own.at[:, columns], win.at[:, pl.ds(h * tile, tile)], far_s.at[1 + h], far_r.at[1 + h], r, far_col
        )

    def nout_far():
        return remote(nout_send, nout, far_s.at[3], far_r.at[3], r, far_col)

    krs = (part, k_ra1, k_ra2, k_rb1, k_rb2, k_sa, k_sb, krs_s, krs_r)
    qrs = (direct, q_ra1, q_ra2, q_rb1, q_rb2, q_sa, q_sb, qrs_s, qrs_r)

    partial_keys(0)
    pl.semaphore_wait(barrier, 14 + jnp.where(r > 0, NROW, 0) - jnp.where(is_mid, 2, 0))
    for d in range(1, NX):
        rs_a1(part, k_ra1, krs_s, krs_r, d).start()
    partial_keys(1)
    rs_b1(part, k_rb1, krs_s, krs_r).start()

    slab_copy.wait()

    @pl.when(low)
    def _():
        add_rows(slab_send, 0, far_rows, [(slab_f, 0)])
        slab_far().start()

    for i in range(tiles):
        cov_copy(i).wait()
        add_rows(cov, i * tile, tile, [(cov_f, i * tile)])

    @pl.when(jnp.logical_not(low))
    def _():
        slab_pad[...] = jnp.zeros_like(slab_pad)
        add_rows(slab_pad, tile + at_1 - start_1, far_rows, [(slab_f, 0)])

    rs_middle(*krs)
    rs_end(k_ra2, k_rb2, k_sa, k_sb, krs_s, krs_r, own, [], [])
    for h in range(2):
        relay_copy(h, 0).start()

    @pl.when(u > 0)
    def _():
        for h in range(2):
            relay_copy(h, 1).start()

    ag_start(own, kag_s, kag_r)
    ag_middle(own, kag_s, kag_r)

    def own_on(i):
        for h in range(2):
            lag_copy(h, r, i, own.at[chunk(h, r)]).start()

    def relay_on(far):
        def send(i):
            for h in range(2):
                lag_copy(h, r, i, relay.at[far, h]).start()

        return send

    each(1, PLANE - u, own_on)
    for h in range(2):
        relay_copy(h, 0).wait_recv()
    others(PLANE - u, 2 * PLANE - u, relay_on(0))

    @pl.when(is_mid)
    def _():
        for h in range(2):
            lag_stay(h, relay.at[0, h]).start()

    @pl.when(u > 0)
    def _():
        for h in range(2):
            relay_copy(h, 1).wait_recv()
        each(2 * PLANE - u, NROW, relay_on(1))

    @pl.when(jnp.logical_not(low))
    def _():
        slab_far().wait_recv()
        add_rows(slab_pad, at_0 - start_0, far_rows, [(slab_in, 0)])

    ag_end(own, kag_s, kag_r)

    @pl.when(low)
    def _():
        win_far(0).start()
        win_far(1).start()

    contract_last = (((1,), (1,)), ((), ()))

    @pl.when(r > 0)
    def _():
        def mirror(n):
            block = pl.ds(pl.multiple_of(n * tile, tile), tile)
            mir[:, block] = lax.dot_general(
                own[...], cov[block, :], contract_last, preferred_element_type=F32
            ).astype(BF16)

        each(0, tiles, mirror)

        def send_mir(e):
            for h in range(2):
                mir_copy(h, e, r - 1).start()

        others(0, NROW, send_mir)

    @pl.when(is_mid)
    def _():
        for h in range(2):
            mir_stay(h).start()

    @pl.when(jnp.logical_not(low))
    def _():
        def narrow(n):
            block = pl.ds(pl.multiple_of(n * tile, tile), tile)
            nout_send[:, block] = lax.dot_general(
                own[...], slab_pad[block, :], contract_last, preferred_element_type=F32
            ).astype(BF16)

        each(0, 2, narrow)
        nout_far().start()

    own_to_lag = pltpu.make_async_copy(own, lag, loc_sem)

    @pl.when(r == 0)
    def _():
        own_to_lag.start()
        own_to_lag.wait()

    @pl.when(r > 0)
    def _():
        def got_lag(e):
            for h in range(2):
                lag_copy(h, e, 1, own.at[chunk(h, r)]).wait_recv()

        others(0, NROW, got_lag)

    @pl.when(is_mid)
    def _():
        for h in range(2):
            lag_stay(h, relay.at[0, h]).wait()

    @pl.when(low)
    def _():
        def step(n):
            block = pl.ds(pl.multiple_of(n * tile, tile), tile)
            direct[:, block] = jnp.dot(
                lag[...], cov[:, block], preferred_element_type=F32
            ).astype(BF16)

        each(0, tiles, step)
        nout_far().wait_recv()

        def add_narrow(i):
            rows = pl.ds(pl.multiple_of(i * 64, 64), 64)
            for h, start in ((0, start_0), (1, start_1)):
                columns = pl.ds(start, tile)
                direct[rows, columns] = (
                    direct[rows, columns].astype(F32)
                    + nout[rows, pl.ds(h * tile, tile)].astype(F32)
                ).astype(BF16)

        each(0, edits // 64, add_narrow)

    @pl.when(jnp.logical_not(low))
    def _():
        win_far(0).wait_recv()
        win_far(1).wait_recv()

        def step(n):
            block = pl.ds(pl.multiple_of(n * tile, tile), tile)
            direct[:, block] = (
                jnp.dot(lag[...], cov[:, block], preferred_element_type=F32)
                + jnp.dot(win[...], slab_pad[:, block], preferred_element_type=F32)
            ).astype(BF16)

        each(0, tiles, step)

    for d in range(1, NX):
        rs_a1(direct, q_ra1, qrs_s, qrs_r, d).start()
    rs_b1(direct, q_rb1, qrs_s, qrs_r).start()

    def got_mir(i):
        for h in range(2):
            mir_copy(h, r, i - 1).wait_recv()

    others(1, NROW, got_mir)

    @pl.when(is_mid)
    def _():
        for h in range(2):
            mir_stay(h).wait()

    add_slots(crossed.at[0], 0, PLANE - u - 1, 2 * PLANE - u - 1)
    cross_copy(0).start()

    @pl.when(u > 0)
    def _():
        add_slots(crossed.at[1], 0, 2 * PLANE - u - 1, NROW - 1)
        cross_copy(1).start()

    add_slots(q_sum, 0, 0, PLANE - u - 1)
    rs_middle(*qrs)
    cross_copy(0).wait_recv()
    add_rows(q_sum, 0, 2 * ch, [(q_sum, 0), (cross_in.at[0], 0)])

    @pl.when(u > 0)
    def _():
        cross_copy(1).wait_recv()
        add_rows(q_sum, 0, 2 * ch, [(q_sum, 0), (cross_in.at[1], 0)])

    rs_end(q_ra2, q_rb2, q_sa, q_sb, qrs_s, qrs_r, q_all, [(q_sum, 0)], [(q_sum, ch)])
    ag_start(q_all, qag_s, qag_r)
    ag_middle(q_all, qag_s, qag_r)
    ag_end(q_all, qag_s, qag_r)
    result = pltpu.make_async_copy(q_all, out_ref, loc_sem)
    result.start()

    rs_sent(*krs)
    rs_sent(*qrs)
    ag_sent(own, kag_s, kag_r)
    ag_sent(q_all, qag_s, qag_r)

    def lag_sent(i):
        for h in range(2):
            lag_copy(h, r, i, own.at[chunk(h, r)]).wait_send()

    others(1, NROW, lag_sent)

    @pl.when(r > 0)
    def _():
        def mir_sent(e):
            for h in range(2):
                mir_copy(h, e, r - 1).wait_send()

        others(0, NROW, mir_sent)

    for h in range(2):
        relay_copy(h, 0).wait_send()
    cross_copy(0).wait_send()

    @pl.when(u > 0)
    def _():
        for h in range(2):
            relay_copy(h, 1).wait_send()
        cross_copy(1).wait_send()

    @pl.when(low)
    def _():
        slab_far().wait_send()
        win_far(0).wait_send()
        win_far(1).wait_send()

    @pl.when(jnp.logical_not(low))
    def _():
        nout_far().wait_send()

    result.wait()


def delta_kernel(residual_ref, q_ref, out_ref):
    out_ref[...] = jnp.dot(residual_ref[...], q_ref[...], preferred_element_type=F32).astype(
        out_ref.dtype
    )


def shards(tokens, edit_src, cov_tiles, cov_far, residual):
    edits = edit_src.shape[0]
    tok_dev, width = tokens.shape
    ch = edits // 2 // NROW
    far_rows = cov_far.shape[1]
    tiles = width // 256

    def buf(*shape, dtype=BF16):
        return pltpu.VMEM(shape, dtype)

    def dma(*shape):
        return pltpu.SemaphoreType.DMA(shape)

    def reduce_bufs():
        return [
            buf(NX - 1, 2 * ch, width), buf(ch, width), buf(NX * ch, width),
            buf(NX - 1, ch, width), buf(2 * ch, width), buf(NX * ch, width),
        ]

    q_block = pl.pallas_call(
        kernel,
        name="edit_product",
        out_shape=jax.ShapeDtypeStruct((edits, width), BF16),
        in_specs=[
            pl.BlockSpec(memory_space=pltpu.VMEM),
            pl.BlockSpec(memory_space=pltpu.VMEM),
            pl.BlockSpec(memory_space=pl.ANY),
            pl.BlockSpec(memory_space=pl.ANY),
        ],
        out_specs=pl.BlockSpec(memory_space=pl.ANY),
        scratch_shapes=[
            buf(edits, tok_dev), buf(edits, width),
            buf(width, width, dtype=F32), buf(width, width),
            buf(far_rows, width, dtype=F32), buf(far_rows, width), buf(far_rows, width), buf(512, width),
            buf(edits, width), buf(edits, width), buf(edits, width), buf(edits, width),
            buf(edits, 512), buf(edits, 512), buf(edits, 512),
            *reduce_bufs(),
            *reduce_bufs(),
            buf(NROW - 1, 2, ch, width), buf(2 * ch, width, dtype=F32), buf(edits, width),
            buf(2, 2, ch, width), buf(2, 2 * ch, width), buf(2, 2 * ch, width),
            dma(tiles), pltpu.SemaphoreType.DMA, pltpu.SemaphoreType.DMA,
            dma(8), dma(8), dma(8), dma(8), dma(8), dma(8), dma(8), dma(8),
            dma(NROW, 2), dma(NROW, 2), dma(NROW, 2), dma(NROW - 1, 2), dma(4), dma(4),
            dma(2, 2), dma(2, 2), dma(2), dma(2), dma(4),
        ],
        compiler_params=pltpu.CompilerParams(
            collective_id=0, has_side_effects=True, vmem_limit_bytes=60 * 2**20
        ),
    )(edit_src, tokens, cov_tiles, cov_far)

    rows = residual.shape[0]
    step = 256
    return pl.pallas_call(
        delta_kernel,
        name="delta",
        grid=(rows // step,),
        out_shape=jax.ShapeDtypeStruct((rows, width), BF16),
        in_specs=[
            pl.BlockSpec((step, edits), lambda i: (i, 0)),
            pl.BlockSpec((edits, width), lambda i: (0, 0)),
        ],
        out_specs=pl.BlockSpec((step, width), lambda i: (i, 0)),
        compiler_params=pltpu.CompilerParams(vmem_limit_bytes=32 * 2**20),
    )(residual, q_block)


def solution(mesh):
    placed = (
        P("row", "col"),
        P(),
        P("row", "col", None, None),
        P("col", "row", None),
        P("row", None),
    )
    return jax.shard_map(
        shards, mesh=mesh, in_specs=placed, out_specs=P("row", "col"), check_vma=False
    )
```

```python
import functools

import jax
import jax.numpy as jnp
from jax import lax
from jax.experimental import pallas as pl
from jax.experimental.pallas import tpu as pltpu
from jax.sharding import PartitionSpec as P

MESH = pl.DeviceIdType.MESH
F32 = jnp.float32
BF16 = jnp.bfloat16
NX = 4
NROW = 8
NCOL = 16
PLANE = 4
GROUPS = 2
SLAB = 16


def remote(src, dst, send_sem, recv_sem, row, col):
    return pltpu.make_async_remote_copy(
        src_ref=src,
        dst_ref=dst,
        send_sem=send_sem,
        recv_sem=recv_sem,
        device_id=(row, col),
        device_id_type=MESH,
    )


def add_rows(out_ref, out_at, rows, terms):
    def step(i, carry):
        at = pl.multiple_of(i * SLAB, SLAB)
        total = None
        for ref, start in terms:
            part = ref[pl.ds(pl.multiple_of(start + at, SLAB), SLAB), :].astype(F32)
            total = part if total is None else total + part
        out_ref[pl.ds(pl.multiple_of(out_at + at, SLAB), SLAB), :] = total.astype(out_ref.dtype)
        return carry

    lax.fori_loop(0, rows // SLAB, step, 0)


def kernel(
    edit_ref, tok_ref, cov_ref, far_ref, out_ref,
    counts, part, cov_f, cov, slab_f, slab_send, slab_in, slab_pad,
    own, lag, mir, direct, win, nout_send, nout,
    k_ra1, k_ra2, k_rb1, k_rb2, k_sa, k_sb,
    q_ra1, q_ra2, q_rb1, q_rb2, q_sa, q_sb, m_in, q_sum, q_all, relay, crossed, cross_in,
    cov_sem, slab_sem, loc_sem, out_sem,
    krs_s, krs_r, kag_s, kag_r, qrs_s, qrs_r, qag_s, qag_r,
    lag_s, lag_r, mir_s, mir_r, slab_s, slab_r, win_s, win_r, nout_s, nout_r,
    rel_s, rel_r, cross_s, cross_r, stay_sem,
):
    r = lax.axis_index("row")
    c = lax.axis_index("col")
    x = r % NX
    yl = r // NX
    ry = (r + NX) % NROW
    edits, width = own.shape
    group = edits // GROUPS
    half = group // 2
    ch = half // NROW
    tok_dev = tok_ref.shape[0]
    tile = 256
    tiles = width // tile
    far_rows = slab_f.shape[0]
    groups = range(GROUPS)

    def across(d):
        return yl * NX + (x + d) % NX

    def behind(d):
        return (x + NX - d) % NX

    u = c % PLANE
    plane = c - u
    is_mid = r == PLANE

    def ahead(i):
        return plane + (u + i) % PLANE

    source_col = plane + (u + NCOL - r) % PLANE
    up_col = (c + PLANE) % NCOL
    down_col = (c + NCOL - PLANE) % NCOL
    low = c < NCOL // 2
    far_col = (c + NCOL // 2) % NCOL

    def chunk_at(g, h, row):
        if h == 0:
            at = (row % NX) * (2 * ch) + (row // NX) * ch
        else:
            at = half + (row // NX) * (NX * ch) + (row % NX) * ch
        return pl.multiple_of(g * group + at, ch)

    def chunk(g, h, row):
        return pl.ds(chunk_at(g, h, row), ch)

    def each(low_end, high_end, do):
        def step(i, carry):
            do(i)
            return carry

        lax.fori_loop(low_end, high_end, step, 0)

    def others(low_end, high_end, do):
        def step(i):
            @pl.when(jnp.logical_not(jnp.logical_and(is_mid, i == PLANE)))
            def _():
                do(i)

        each(low_end, high_end, step)

    barrier = pltpu.get_barrier_semaphore()

    def greet(row, col):
        pl.semaphore_signal(barrier, inc=1, device_id=(row, col), device_id_type=MESH)

    for d in range(1, NX):
        greet(across(d), c)
    greet(ry, c)
    greet(r, far_col)
    greet(r, up_col)
    greet(r, down_col)
    others(1, NROW, lambda i: greet(i, ahead(i)))

    @pl.when(r > 0)
    def _():
        others(0, NROW, lambda e: greet(e, source_col))

    def cov_copy(i):
        rows = pl.ds(i * tile, tile)
        return pltpu.make_async_copy(cov_ref.at[0, 0, rows], cov_f.at[rows], cov_sem.at[i])

    def cov_ready(i):
        cov_copy(i).wait()
        add_rows(cov, i * tile, tile, [(cov_f, i * tile)])

    slab_copy = pltpu.make_async_copy(far_ref.at[0], slab_f, slab_sem)
    slab_copy.start()
    for i in range(tiles):
        cov_copy(i).start()

    def partial_keys(g):
        for at in range(g * group, (g + 1) * group, 128):
            relative = edit_ref[:, at : at + 128] - r * tok_dev
            slots = lax.broadcasted_iota(jnp.int32, (tok_dev, 128), 0)
            total = jnp.zeros((tok_dev, 128), F32)
            for j in range(edit_ref.shape[0]):
                total = total + (relative[j : j + 1, :] == slots).astype(F32)
            counts[at : at + 128, :] = (total / edit_ref.shape[0]).T.astype(BF16)

        def step(n):
            columns = pl.ds(pl.multiple_of(n * tile, tile), tile)
            part[pl.ds(g * group, group), columns] = jnp.dot(
                counts[pl.ds(g * group, group), :], tok_ref[:, columns], preferred_element_type=F32
            ).astype(BF16)

        each(0, tiles, step)

    class Scatter:
        def __init__(self, src, ra1, ra2, rb1, rb2, sa, sb, ss, rs):
            self.src, self.ra1, self.ra2, self.rb1, self.rb2 = src, ra1, ra2, rb1, rb2
            self.sa, self.sb, self.ss, self.rs = sa, sb, ss, rs

        def a1(self, g, d):
            rows = pl.ds(pl.multiple_of(g * group + ((x + d) % NX) * (2 * ch), 2 * ch), 2 * ch)
            return remote(
                self.src.at[rows], self.ra1.at[g, d - 1], self.ss.at[g, d - 1], self.rs.at[g, d - 1], across(d), c
            )

        def b1(self, g):
            rows = pl.ds(pl.multiple_of(g * group + half + (1 - yl) * (NX * ch), NX * ch), NX * ch)
            return remote(self.src.at[rows], self.rb1.at[g], self.ss.at[g, 3], self.rs.at[g, 3], ry, c)

        def a2(self, g):
            rows = pl.ds(pl.multiple_of((1 - yl) * ch, ch), ch)
            return remote(self.sa.at[g, rows], self.ra2.at[g], self.ss.at[g, 4], self.rs.at[g, 4], ry, c)

        def b2(self, g, d):
            rows = pl.ds(pl.multiple_of(((x + d) % NX) * ch, ch), ch)
            return remote(
                self.sb.at[g, rows], self.rb2.at[g, d - 1], self.ss.at[g, 4 + d], self.rs.at[g, 4 + d], across(d), c
            )

        def start(self, g):
            for d in (1, 3, 2):
                self.a1(g, d).start()
            self.b1(g).start()

        def middle(self, g):
            self.b1(g).wait_recv()
            add_rows(
                self.sb.at[g], 0, NX * ch, [(self.src, g * group + half + yl * (NX * ch)), (self.rb1.at[g], 0)]
            )
            for d in (1, 3, 2):
                self.b2(g, d).start()
            for d in range(1, NX):
                self.a1(g, d).wait_recv()
            add_rows(
                self.sa.at[g], 0, 2 * ch,
                [(self.src, g * group + x * (2 * ch))] + [(self.ra1.at[g, d], 0) for d in range(NX - 1)],
            )
            self.a2(g).start()

        def end(self, g, out, a_more, b_more):
            self.a2(g).wait_recv()
            add_rows(out, chunk_at(g, 0, r), ch, [(self.sa.at[g], yl * ch), (self.ra2.at[g], 0)] + a_more)
            for d in range(1, NX):
                self.b2(g, d).wait_recv()
            add_rows(
                out, chunk_at(g, 1, r), ch,
                [(self.sb.at[g], x * ch)] + [(self.rb2.at[g, d], 0) for d in range(NX - 1)] + b_more,
            )

        def sent(self, g):
            self.b1(g).wait_send()
            self.a2(g).wait_send()
            for d in range(1, NX):
                self.a1(g, d).wait_send()
                self.b2(g, d).wait_send()

    class Gather:
        def __init__(self, full, ss, rs):
            self.full, self.ss, self.rs = full, ss, rs

        def move(self, g, rows, sem, row):
            return remote(
                self.full.at[rows], self.full.at[rows], self.ss.at[g, sem], self.rs.at[g, sem], row, c
            )

        def a1(self, g, row):
            return self.move(g, chunk(g, 0, row), 0, ry)

        def b1(self, g, row, d):
            return self.move(g, chunk(g, 1, row), d, across(d))

        def a2(self, g, xx, d):
            rows = pl.ds(pl.multiple_of(g * group + xx * (2 * ch), 2 * ch), 2 * ch)
            return self.move(g, rows, 3 + d, across(d))

        def b2(self, g, yy):
            rows = pl.ds(pl.multiple_of(g * group + half + yy * (NX * ch), NX * ch), NX * ch)
            return self.move(g, rows, 7, ry)

        def start(self, g):
            self.a1(g, r).start()
            for d in (1, 3, 2):
                self.b1(g, r, d).start()

        def middle(self, g):
            self.a1(g, ry).wait_recv()
            for d in (1, 3, 2):
                self.a2(g, x, d).start()
            for d in range(1, NX):
                self.b1(g, yl * NX + behind(d), d).wait_recv()
            self.b2(g, yl).start()

        def end(self, g):
            for d in range(1, NX):
                self.a2(g, behind(d), d).wait_recv()
            self.b2(g, 1 - yl).wait_recv()

        def sent(self, g):
            self.a1(g, r).wait_send()
            for d in range(1, NX):
                self.b1(g, r, d).wait_send()
                self.a2(g, x, d).wait_send()
            self.b2(g, yl).wait_send()

    def relay_copy(g, h, far):
        return remote(
            own.at[chunk(g, h, r)], relay.at[far, g, h], rel_s.at[far, g, h], rel_r.at[far, g, h], r,
            far_col if far else up_col,
        )

    def lag_copy(g, h, source, i, held):
        return remote(
            held, lag.at[chunk(g, h, source)], lag_s.at[i, g, h], lag_r.at[source, g, h], i, ahead(i)
        )

    def own_on(g, h):
        def send(i):
            lag_copy(g, h, r, i, own.at[chunk(g, h, r)]).start()

        return send

    def relay_on(g, h, far):
        def send(i):
            lag_copy(g, h, r, i, relay.at[far, g, h]).start()

        return send

    def lag_stay(g, h):
        return pltpu.make_async_copy(relay.at[0, g, h], lag.at[chunk(g, h, r)], stay_sem.at[0, g, h])

    def mir_copy(g, h, e, slot):
        return remote(
            mir.at[chunk(g, h, e)], m_in.at[slot, g, h], mir_s.at[e, g, h], mir_r.at[slot, g, h], e, source_col
        )

    def mir_stay(g, h):
        return pltpu.make_async_copy(mir.at[chunk(g, h, r)], m_in.at[PLANE - 1, g, h], stay_sem.at[1, g, h])

    def cross_copy(g, far):
        return remote(
            crossed.at[far, g], cross_in.at[far, g], cross_s.at[far, g], cross_r.at[far, g], r,
            far_col if far else down_col,
        )

    def add_slots(out, g, first, last):
        for h in range(2):
            for at in range(0, ch, SLAB):
                rows = pl.ds(at, SLAB)
                total = lax.fori_loop(
                    first, last,
                    lambda slot, so_far: so_far + m_in[slot, g, h, rows, :].astype(F32),
                    jnp.zeros((SLAB, width), F32),
                )
                out[pl.ds(h * ch + at, SLAB), :] = total.astype(out.dtype)

    at_0 = r * far_rows
    at_1 = width // 2 + r * far_rows
    start_0 = pl.multiple_of(at_0 // 128 * 128, 128)
    start_1 = pl.multiple_of(jnp.minimum(at_1 // 128 * 128, width - tile), 128)

    def rows_of(g):
        return pl.ds(g * group, group)

    def slab_far():
        return remote(slab_send, slab_in, slab_s, slab_r, r, far_col)

    def win_far(g, h):
        columns = pl.ds(start_0 if h == 0 else start_1, tile)
        return remote(
            own.at[rows_of(g), columns], win.at[rows_of(g), pl.ds(h * tile, tile)],
            win_s.at[g, h], win_r.at[g, h], r, far_col,
        )

    def nout_far(g):
        return remote(nout_send.at[rows_of(g)], nout.at[rows_of(g)], nout_s.at[g], nout_r.at[g], r, far_col)

    k_scatter = Scatter(part, k_ra1, k_ra2, k_rb1, k_rb2, k_sa, k_sb, krs_s, krs_r)
    q_scatter = Scatter(direct, q_ra1, q_ra2, q_rb1, q_rb2, q_sa, q_sb, qrs_s, qrs_r)
    k_gather = Gather(own, kag_s, kag_r)
    q_gather = Gather(q_all, qag_s, qag_r)
    contract_last = (((1,), (1,)), ((), ()))

    partial_keys(0)
    pl.semaphore_wait(barrier, 14 + jnp.where(r > 0, NROW, 0) - jnp.where(is_mid, 2, 0))
    k_scatter.start(0)
    for g in range(1, GROUPS):
        partial_keys(g)
        k_scatter.start(g)

    slab_copy.wait()

    @pl.when(low)
    def _():
        add_rows(slab_send, 0, far_rows, [(slab_f, 0)])
        slab_far().start()

    for i in range(2):
        cov_ready(i)
    for g in groups:
        k_scatter.middle(g)
    for i in range(2, 4):
        cov_ready(i)

    for g in groups:
        k_scatter.end(g, own, [], [])
        k_gather.start(g)
        for h in range(2):
            relay_copy(g, h, 0).start()

        @pl.when(u > 0)
        def _(g=g):
            for h in range(2):
                relay_copy(g, h, 1).start()

    for g in groups:
        k_gather.middle(g)
        for h in range(2):
            each(1, PLANE - u, own_on(g, h))

    for g in groups:
        for h in range(2):
            relay_copy(g, h, 0).wait_recv()
            others(PLANE - u, 2 * PLANE - u, relay_on(g, h, 0))

        @pl.when(is_mid)
        def _(g=g):
            for h in range(2):
                lag_stay(g, h).start()

        @pl.when(u > 0)
        def _(g=g):
            for h in range(2):
                relay_copy(g, h, 1).wait_recv()
                each(2 * PLANE - u, NROW, relay_on(g, h, 1))

    for i in range(4, tiles):
        cov_ready(i)

    @pl.when(jnp.logical_not(low))
    def _():
        slab_pad[...] = jnp.zeros_like(slab_pad)
        add_rows(slab_pad, tile + at_1 - start_1, far_rows, [(slab_f, 0)])
        slab_far().wait_recv()
        add_rows(slab_pad, at_0 - start_0, far_rows, [(slab_in, 0)])

    for g in groups:
        k_gather.end(g)

        @pl.when(low)
        def _(g=g):
            for h in range(2):
                win_far(g, h).start()

        @pl.when(r > 0)
        def _(g=g):
            def mirror(n):
                block = pl.ds(pl.multiple_of(n * tile, tile), tile)
                mir[rows_of(g), block] = lax.dot_general(
                    own[rows_of(g), :], cov[block, :], contract_last, preferred_element_type=F32
                ).astype(BF16)

            each(0, tiles, mirror)

            for h in range(2):
                others(0, NROW, lambda e, h=h: mir_copy(g, h, e, r - 1).start())

        @pl.when(is_mid)
        def _(g=g):
            for h in range(2):
                mir_stay(g, h).start()

        @pl.when(jnp.logical_not(low))
        def _(g=g):
            def narrow(n):
                block = pl.ds(pl.multiple_of(n * tile, tile), tile)
                nout_send[rows_of(g), block] = lax.dot_general(
                    own[rows_of(g), :], slab_pad[block, :], contract_last, preferred_element_type=F32
                ).astype(BF16)

            each(0, 2, narrow)
            nout_far(g).start()

    for g in groups:
        own_to_lag = pltpu.make_async_copy(own.at[rows_of(g)], lag.at[rows_of(g)], loc_sem)

        @pl.when(r == 0)
        def _(own_to_lag=own_to_lag):
            own_to_lag.start()
            own_to_lag.wait()

        @pl.when(r > 0)
        def _(g=g):
            def got_lag(e):
                for h in range(2):
                    lag_copy(g, h, e, 1, own.at[chunk(g, h, r)]).wait_recv()

            others(0, NROW, got_lag)

        @pl.when(is_mid)
        def _(g=g):
            for h in range(2):
                lag_stay(g, h).wait()

        @pl.when(low)
        def _(g=g):
            def step(n):
                block = pl.ds(pl.multiple_of(n * tile, tile), tile)
                direct[rows_of(g), block] = jnp.dot(
                    lag[rows_of(g), :], cov[:, block], preferred_element_type=F32
                ).astype(BF16)

            each(0, tiles, step)
            nout_far(g).wait_recv()

            def add_narrow(i):
                rows = pl.ds(pl.multiple_of(g * group + i * 64, 64), 64)
                for h, start in ((0, start_0), (1, start_1)):
                    columns = pl.ds(start, tile)
                    direct[rows, columns] = (
                        direct[rows, columns].astype(F32)
                        + nout[rows, pl.ds(h * tile, tile)].astype(F32)
                    ).astype(BF16)

            each(0, group // 64, add_narrow)

        @pl.when(jnp.logical_not(low))
        def _(g=g):
            for h in range(2):
                win_far(g, h).wait_recv()

            def step(n):
                block = pl.ds(pl.multiple_of(n * tile, tile), tile)
                direct[rows_of(g), block] = (
                    jnp.dot(lag[rows_of(g), :], cov[:, block], preferred_element_type=F32)
                    + jnp.dot(win[rows_of(g), :], slab_pad[:, block], preferred_element_type=F32)
                ).astype(BF16)

            each(0, tiles, step)

        q_scatter.start(g)

    for g in groups:
        def got_mir(i, g=g):
            for h in range(2):
                mir_copy(g, h, r, i - 1).wait_recv()

        others(1, NROW, got_mir)

        @pl.when(is_mid)
        def _(g=g):
            for h in range(2):
                mir_stay(g, h).wait()

        add_slots(crossed.at[0, g], g, PLANE - u - 1, 2 * PLANE - u - 1)
        cross_copy(g, 0).start()

        @pl.when(u > 0)
        def _(g=g):
            add_slots(crossed.at[1, g], g, 2 * PLANE - u - 1, NROW - 1)
            cross_copy(g, 1).start()

        add_slots(q_sum.at[g], g, 0, PLANE - u - 1)
        q_scatter.middle(g)

    for g in groups:
        cross_copy(g, 0).wait_recv()
        total = q_sum.at[g]
        add_rows(total, 0, 2 * ch, [(total, 0), (cross_in.at[0, g], 0)])

        @pl.when(u > 0)
        def _(g=g, total=total):
            cross_copy(g, 1).wait_recv()
            add_rows(total, 0, 2 * ch, [(total, 0), (cross_in.at[1, g], 0)])

        q_scatter.end(g, q_all, [(total, 0)], [(total, ch)])
        q_gather.start(g)

    def result(g):
        return pltpu.make_async_copy(q_all.at[rows_of(g)], out_ref.at[rows_of(g)], out_sem.at[g])

    for g in groups:
        q_gather.middle(g)
    for g in groups:
        q_gather.end(g)
        result(g).start()

    for g in groups:
        k_scatter.sent(g)
        q_scatter.sent(g)
        k_gather.sent(g)
        q_gather.sent(g)

        def lag_sent(i, g=g):
            for h in range(2):
                lag_copy(g, h, r, i, own.at[chunk(g, h, r)]).wait_send()

        others(1, NROW, lag_sent)

        @pl.when(r > 0)
        def _(g=g):
            def mir_sent(e):
                for h in range(2):
                    mir_copy(g, h, e, r - 1).wait_send()

            others(0, NROW, mir_sent)

        for h in range(2):
            relay_copy(g, h, 0).wait_send()
        cross_copy(g, 0).wait_send()

        @pl.when(u > 0)
        def _(g=g):
            for h in range(2):
                relay_copy(g, h, 1).wait_send()
            cross_copy(g, 1).wait_send()

        @pl.when(low)
        def _(g=g):
            for h in range(2):
                win_far(g, h).wait_send()

        @pl.when(jnp.logical_not(low))
        def _(g=g):
            nout_far(g).wait_send()

    @pl.when(low)
    def _():
        slab_far().wait_send()

    for g in groups:
        result(g).wait()


def delta_kernel(residual_ref, q_ref, out_ref):
    out_ref[...] = jnp.dot(residual_ref[...], q_ref[...], preferred_element_type=F32).astype(
        out_ref.dtype
    )


def shards(tokens, edit_src, cov_tiles, cov_far, residual):
    edits, context = edit_src.shape
    tok_dev, width = tokens.shape
    ch = edits // GROUPS // 2 // NROW
    far_rows = cov_far.shape[1]
    tiles = width // 256

    def buf(*shape, dtype=BF16):
        return pltpu.VMEM(shape, dtype)

    def dma(*shape):
        return pltpu.SemaphoreType.DMA(shape)

    def reduce_bufs():
        return [
            buf(GROUPS, NX - 1, 2 * ch, width), buf(GROUPS, ch, width), buf(GROUPS, NX * ch, width),
            buf(GROUPS, NX - 1, ch, width), buf(GROUPS, 2 * ch, width), buf(GROUPS, NX * ch, width),
        ]

    q_block = pl.pallas_call(
        kernel,
        name="edit_product",
        out_shape=jax.ShapeDtypeStruct((edits, width), BF16),
        in_specs=[
            pl.BlockSpec(memory_space=pltpu.VMEM),
            pl.BlockSpec(memory_space=pltpu.VMEM),
            pl.BlockSpec(memory_space=pl.ANY),
            pl.BlockSpec(memory_space=pl.ANY),
        ],
        out_specs=pl.BlockSpec(memory_space=pl.ANY),
        scratch_shapes=[
            buf(edits, tok_dev), buf(edits, width),
            buf(width, width, dtype=F32), buf(width, width),
            buf(far_rows, width, dtype=F32), buf(far_rows, width), buf(far_rows, width), buf(512, width),
            buf(edits, width), buf(edits, width), buf(edits, width), buf(edits, width),
            buf(edits, 512), buf(edits, 512), buf(edits, 512),
            *reduce_bufs(),
            *reduce_bufs(),
            buf(NROW - 1, GROUPS, 2, ch, width), buf(GROUPS, 2 * ch, width, dtype=F32), buf(edits, width),
            buf(2, GROUPS, 2, ch, width), buf(2, GROUPS, 2 * ch, width), buf(2, GROUPS, 2 * ch, width),
            dma(tiles), pltpu.SemaphoreType.DMA, pltpu.SemaphoreType.DMA, dma(GROUPS),
            *[dma(GROUPS, 8) for _ in range(8)],
            dma(NROW, GROUPS, 2), dma(NROW, GROUPS, 2), dma(NROW, GROUPS, 2), dma(NROW - 1, GROUPS, 2),
            pltpu.SemaphoreType.DMA, pltpu.SemaphoreType.DMA,
            dma(GROUPS, 2), dma(GROUPS, 2), dma(GROUPS), dma(GROUPS),
            dma(2, GROUPS, 2), dma(2, GROUPS, 2), dma(2, GROUPS), dma(2, GROUPS), dma(2, GROUPS, 2),
        ],
        compiler_params=pltpu.CompilerParams(
            collective_id=0, has_side_effects=True, vmem_limit_bytes=60 * 2**20
        ),
    )(edit_src.T, tokens, cov_tiles, cov_far)

    rows = residual.shape[0]
    step = 256
    return pl.pallas_call(
        delta_kernel,
        name="delta",
        grid=(rows // step,),
        out_shape=jax.ShapeDtypeStruct((rows, width), BF16),
        in_specs=[
            pl.BlockSpec((step, edits), lambda i: (i, 0)),
            pl.BlockSpec((edits, width), lambda i: (0, 0)),
        ],
        out_specs=pl.BlockSpec((step, width), lambda i: (i, 0)),
        compiler_params=pltpu.CompilerParams(vmem_limit_bytes=32 * 2**20),
    )(residual, q_block)


def solution(mesh):
    placed = (
        P("row", "col"),
        P(),
        P("row", "col", None, None),
        P("col", "row", None),
        P("row", None),
    )
    return jax.shard_map(
        shards, mesh=mesh, in_specs=placed, out_specs=P("row", "col"), check_vma=False
    )
```

```python
import functools

import jax
import jax.numpy as jnp
from jax import lax
from jax.experimental import pallas as pl
from jax.experimental.pallas import tpu as pltpu
from jax.sharding import PartitionSpec as P

MESH = pl.DeviceIdType.MESH
F32 = jnp.float32
BF16 = jnp.bfloat16
NX = 4
NROW = 8
NCOL = 16
PLANE = 4
GROUPS = 2
SLAB = 16


def remote(src, dst, send_sem, recv_sem, row, col):
    return pltpu.make_async_remote_copy(
        src_ref=src,
        dst_ref=dst,
        send_sem=send_sem,
        recv_sem=recv_sem,
        device_id=(row, col),
        device_id_type=MESH,
    )


def add_rows(out_ref, out_at, rows, terms):
    def step(i, carry):
        at = pl.multiple_of(i * SLAB, SLAB)
        total = None
        for ref, start in terms:
            part = ref[pl.ds(pl.multiple_of(start + at, SLAB), SLAB), :].astype(F32)
            total = part if total is None else total + part
        out_ref[pl.ds(pl.multiple_of(out_at + at, SLAB), SLAB), :] = total.astype(out_ref.dtype)
        return carry

    lax.fori_loop(0, rows // SLAB, step, 0)


def kernel(
    edit_ref, tok_ref, cov_ref, far_ref, out_ref,
    counts, part, cov_f, cov, slab_f, slab_send, slab_in, slab_pad,
    own, lag, mir, direct, win, nout_send, nout,
    k_ra1, k_ra2, k_rb1, k_rb2, k_sa, k_sb,
    q_ra1, q_ra2, q_rb1, q_rb2, q_sa, q_sb, m_in, q_sum, q_all, held, mid, crossed, cross_in,
    cov_sem, slab_sem, loc_sem, out_sem,
    krs_s, krs_r, kag_s, kag_r, qrs_s, qrs_r, qag_s, qag_r,
    first_s, first_r, second_s, second_r, mir_s, mir_r, slab_s, slab_r, win_s, win_r, nout_s, nout_r,
    rel_s, rel_r, cross_s, cross_r, stay_sem, keep_sem,
):
    r = lax.axis_index("row")
    c = lax.axis_index("col")
    x = r % NX
    yl = r // NX
    ry = (r + NX) % NROW
    edits, width = own.shape
    group = edits // GROUPS
    half = group // 2
    ch = half // NROW
    tok_dev = tok_ref.shape[0]
    tile = 256
    tiles = width // tile
    far_rows = slab_f.shape[0]
    groups = range(GROUPS)

    def across(d):
        return yl * NX + (x + d) % NX

    def behind(d):
        return (x + NX - d) % NX

    u = c % PLANE
    plane = c - u
    is_mid = r == PLANE

    def ahead(i):
        return plane + (u + i) % PLANE

    source_col = plane + (u + NCOL - r) % PLANE
    up_col = (c + PLANE) % NCOL
    down_col = (c + NCOL - PLANE) % NCOL
    low = c < NCOL // 2
    far_col = (c + NCOL // 2) % NCOL

    def chunk_at(g, h, row):
        if h == 0:
            at = (row % NX) * (2 * ch) + (row // NX) * ch
        else:
            at = half + (row // NX) * (NX * ch) + (row % NX) * ch
        return pl.multiple_of(g * group + at, ch)

    def chunk(g, h, row):
        return pl.ds(chunk_at(g, h, row), ch)

    def each(low_end, high_end, do):
        def step(i, carry):
            do(i)
            return carry

        lax.fori_loop(low_end, high_end, step, 0)

    def others(low_end, high_end, do):
        def step(i):
            @pl.when(jnp.logical_not(jnp.logical_and(is_mid, i == PLANE)))
            def _():
                do(i)

        each(low_end, high_end, step)

    barrier = pltpu.get_barrier_semaphore()

    def greet(row, col):
        pl.semaphore_signal(barrier, inc=1, device_id=(row, col), device_id_type=MESH)

    for d in range(1, NX):
        greet(across(d), c)
    greet(ry, c)
    greet(r, far_col)
    greet(r, up_col)
    greet(r, down_col)
    others(1, NROW, lambda i: greet(i, ahead(i)))
    for d in range(NX):
        lag_by = yl * NX + (x + d) % NX

        @pl.when(lag_by > 0)
        def _(lag_by=lag_by):
            greet(x, plane + (u + NROW - lag_by) % PLANE)

            @pl.when(lag_by != PLANE)
            def _():
                greet(NX + x, plane + (u + NROW - lag_by) % PLANE)

    def cov_copy(i):
        rows = pl.ds(i * tile, tile)
        return pltpu.make_async_copy(cov_ref.at[0, 0, rows], cov_f.at[rows], cov_sem.at[i])

    def cov_ready(i):
        cov_copy(i).wait()
        add_rows(cov, i * tile, tile, [(cov_f, i * tile)])

    slab_copy = pltpu.make_async_copy(far_ref.at[0], slab_f, slab_sem)
    slab_copy.start()
    for i in range(tiles):
        cov_copy(i).start()

    def partial_keys(g):
        for at in range(g * group, (g + 1) * group, 128):
            relative = edit_ref[:, at : at + 128] - r * tok_dev
            slots = lax.broadcasted_iota(jnp.int32, (tok_dev, 128), 0)
            total = jnp.zeros((tok_dev, 128), F32)
            for j in range(edit_ref.shape[0]):
                total = total + (relative[j : j + 1, :] == slots).astype(F32)
            counts[at : at + 128, :] = (total / edit_ref.shape[0]).T.astype(BF16)

        def step(n):
            columns = pl.ds(pl.multiple_of(n * tile, tile), tile)
            part[pl.ds(g * group, group), columns] = jnp.dot(
                counts[pl.ds(g * group, group), :], tok_ref[:, columns], preferred_element_type=F32
            ).astype(BF16)

        each(0, tiles, step)

    class Scatter:
        def __init__(self, src, ra1, ra2, rb1, rb2, sa, sb, ss, rs):
            self.src, self.ra1, self.ra2, self.rb1, self.rb2 = src, ra1, ra2, rb1, rb2
            self.sa, self.sb, self.ss, self.rs = sa, sb, ss, rs

        def a1(self, g, d):
            rows = pl.ds(pl.multiple_of(g * group + ((x + d) % NX) * (2 * ch), 2 * ch), 2 * ch)
            return remote(
                self.src.at[rows], self.ra1.at[g, d - 1], self.ss.at[g, d - 1], self.rs.at[g, d - 1], across(d), c
            )

        def b1(self, g):
            rows = pl.ds(pl.multiple_of(g * group + half + (1 - yl) * (NX * ch), NX * ch), NX * ch)
            return remote(self.src.at[rows], self.rb1.at[g], self.ss.at[g, 3], self.rs.at[g, 3], ry, c)

        def a2(self, g):
            rows = pl.ds(pl.multiple_of((1 - yl) * ch, ch), ch)
            return remote(self.sa.at[g, rows], self.ra2.at[g], self.ss.at[g, 4], self.rs.at[g, 4], ry, c)

        def b2(self, g, d):
            rows = pl.ds(pl.multiple_of(((x + d) % NX) * ch, ch), ch)
            return remote(
                self.sb.at[g, rows], self.rb2.at[g, d - 1], self.ss.at[g, 4 + d], self.rs.at[g, 4 + d], across(d), c
            )

        def start(self, g):
            for d in (1, 3, 2):
                self.a1(g, d).start()
            self.b1(g).start()

        def middle(self, g):
            self.b1(g).wait_recv()
            add_rows(
                self.sb.at[g], 0, NX * ch, [(self.src, g * group + half + yl * (NX * ch)), (self.rb1.at[g], 0)]
            )
            for d in (1, 3, 2):
                self.b2(g, d).start()
            for d in range(1, NX):
                self.a1(g, d).wait_recv()
            add_rows(
                self.sa.at[g], 0, 2 * ch,
                [(self.src, g * group + x * (2 * ch))] + [(self.ra1.at[g, d], 0) for d in range(NX - 1)],
            )
            self.a2(g).start()

        def end(self, g, out, a_more, b_more):
            self.a2(g).wait_recv()
            add_rows(out, chunk_at(g, 0, r), ch, [(self.sa.at[g], yl * ch), (self.ra2.at[g], 0)] + a_more)
            for d in range(1, NX):
                self.b2(g, d).wait_recv()
            add_rows(
                out, chunk_at(g, 1, r), ch,
                [(self.sb.at[g], x * ch)] + [(self.rb2.at[g, d], 0) for d in range(NX - 1)] + b_more,
            )

        def sent(self, g):
            self.b1(g).wait_send()
            self.a2(g).wait_send()
            for d in range(1, NX):
                self.a1(g, d).wait_send()
                self.b2(g, d).wait_send()

    class Gather:
        def __init__(self, full, ss, rs):
            self.full, self.ss, self.rs = full, ss, rs

        def move(self, g, rows, sem, row):
            return remote(
                self.full.at[rows], self.full.at[rows], self.ss.at[g, sem], self.rs.at[g, sem], row, c
            )

        def a1(self, g, row):
            return self.move(g, chunk(g, 0, row), 0, ry)

        def b1(self, g, row, d):
            return self.move(g, chunk(g, 1, row), d, across(d))

        def a2(self, g, xx, d):
            rows = pl.ds(pl.multiple_of(g * group + xx * (2 * ch), 2 * ch), 2 * ch)
            return self.move(g, rows, 3 + d, across(d))

        def b2(self, g, yy):
            rows = pl.ds(pl.multiple_of(g * group + half + yy * (NX * ch), NX * ch), NX * ch)
            return self.move(g, rows, 7, ry)

        def start(self, g):
            self.a1(g, r).start()
            for d in (1, 3, 2):
                self.b1(g, r, d).start()

        def middle(self, g):
            self.a1(g, ry).wait_recv()
            for d in (1, 3, 2):
                self.a2(g, x, d).start()
            for d in range(1, NX):
                self.b1(g, yl * NX + behind(d), d).wait_recv()
            self.b2(g, yl).start()

        def end(self, g):
            for d in range(1, NX):
                self.a2(g, behind(d), d).wait_recv()
            self.b2(g, 1 - yl).wait_recv()

        def sent(self, g):
            self.a1(g, r).wait_send()
            for d in range(1, NX):
                self.b1(g, r, d).wait_send()
                self.a2(g, x, d).wait_send()
            self.b2(g, yl).wait_send()

    def relay_copy(g, h, far):
        return remote(
            held.at[0, g, h], held.at[1 + far, g, h], rel_s.at[far, g, h], rel_r.at[far, g, h], r,
            far_col if far else up_col,
        )

    def lag_first(g, h, by, source, from_y):
        y, d = by // NX, (by % NX + NX - x) % NX
        place = mid.at[d, g, h, pl.ds(pl.multiple_of(from_y * ch, ch), ch)]
        return remote(
            source, place, first_s.at[by, g, h], first_r.at[d, from_y, g, h], y * NX + x, ahead(by)
        )

    def lag_stay(g, h):
        return pltpu.make_async_copy(
            held.at[1, g, h], mid.at[(NX - x) % NX, g, h, pl.ds(ch, ch)], keep_sem.at[g, h]
        )

    def here(by):
        return jnp.logical_and(yl == 1, by == PLANE)

    def lag_send(g, level, first, last):
        def send(by):
            @pl.when(jnp.logical_not(here(by)))
            def _():
                for h in range(2):
                    lag_first(g, h, by, held.at[level, g, h], yl).start()

        each(first, last, send)

    def lag_relayed(g):
        for h in range(2):
            relay_copy(g, h, 0).wait_recv()
        lag_send(g, 1, PLANE - u, 2 * PLANE - u)

        @pl.when(yl == 1)
        def _():
            for h in range(2):
                lag_stay(g, h).start()

        @pl.when(u > 0)
        def _():
            for h in range(2):
                relay_copy(g, h, 1).wait_recv()
            lag_send(g, 2, 2 * PLANE - u, NROW)

    def lag_got(g, h, d):
        by = across(d)
        lag_first(g, h, by, held.at[0, g, h], 0).wait_recv()

        @pl.when(here(by))
        def _():
            lag_stay(g, h).wait()

        @pl.when(jnp.logical_not(here(by)))
        def _():
            lag_first(g, h, by, held.at[0, g, h], 1).wait_recv()

    def lag_second(g, d, part_at, xx):
        if part_at == 0:
            source = mid.at[d, g, 0]
            rows = pl.ds(pl.multiple_of(g * group + xx * (2 * ch), 2 * ch), 2 * ch)
        else:
            source = mid.at[d, g, 1, pl.ds((part_at - 1) * ch, ch)]
            rows = chunk(g, 1, (part_at - 1) * NX + xx)
        return remote(
            source, lag.at[rows], second_s.at[d - 1, g, part_at], second_r.at[d - 1, g, part_at], across(d), c
        )

    def passing(d, do):
        @pl.when(across(d) > 0)
        def _():
            do(d)

    def lag_pass(g):
        def on(d):
            for h in range(2):
                lag_got(g, h, d)
                for part_at in (0,) if h == 0 else (1, 2):
                    lag_second(g, d, part_at, x).start()

        for d in (1, 3, 2):
            passing(d, on)

    def lag_sent(g):
        def first_sent(by):
            @pl.when(jnp.logical_not(here(by)))
            def _():
                for h in range(2):
                    lag_first(g, h, by, held.at[0, g, h], yl).wait_send()

        each(1, NROW, first_sent)
        for h in range(2):
            relay_copy(g, h, 0).wait_send()

        @pl.when(u > 0)
        def _():
            for h in range(2):
                relay_copy(g, h, 1).wait_send()

        def on(d):
            for part_at in range(3):
                lag_second(g, d, part_at, x).wait_send()

        for d in range(1, NX):
            passing(d, on)

    def mir_copy(g, h, e, slot):
        return remote(
            mir.at[chunk(g, h, e)], m_in.at[slot, g, h], mir_s.at[e, g, h], mir_r.at[slot, g, h], e, source_col
        )

    def mir_stay(g, h):
        return pltpu.make_async_copy(mir.at[chunk(g, h, r)], m_in.at[PLANE - 1, g, h], stay_sem.at[g, h])

    def cross_copy(g, far):
        return remote(
            crossed.at[far, g], cross_in.at[far, g], cross_s.at[far, g], cross_r.at[far, g], r,
            far_col if far else down_col,
        )

    def add_slots(out, g, first, last):
        for h in range(2):
            for at in range(0, ch, SLAB):
                rows = pl.ds(at, SLAB)
                total = lax.fori_loop(
                    first, last,
                    lambda slot, so_far: so_far + m_in[slot, g, h, rows, :].astype(F32),
                    jnp.zeros((SLAB, width), F32),
                )
                out[pl.ds(h * ch + at, SLAB), :] = total.astype(out.dtype)

    at_0 = r * far_rows
    at_1 = width // 2 + r * far_rows
    start_0 = pl.multiple_of(at_0 // 128 * 128, 128)
    start_1 = pl.multiple_of(jnp.minimum(at_1 // 128 * 128, width - tile), 128)

    def rows_of(g):
        return pl.ds(g * group, group)

    def slab_far():
        return remote(slab_send, slab_in, slab_s, slab_r, r, far_col)

    def win_far(g, h):
        columns = pl.ds(start_0 if h == 0 else start_1, tile)
        return remote(
            own.at[rows_of(g), columns], win.at[rows_of(g), pl.ds(h * tile, tile)],
            win_s.at[g, h], win_r.at[g, h], r, far_col,
        )

    def nout_far(g):
        return remote(nout_send.at[rows_of(g)], nout.at[rows_of(g)], nout_s.at[g], nout_r.at[g], r, far_col)

    k_scatter = Scatter(part, k_ra1, k_ra2, k_rb1, k_rb2, k_sa, k_sb, krs_s, krs_r)
    q_scatter = Scatter(direct, q_ra1, q_ra2, q_rb1, q_rb2, q_sa, q_sb, qrs_s, qrs_r)
    k_gather = Gather(own, kag_s, kag_r)
    q_gather = Gather(q_all, qag_s, qag_r)
    contract_last = (((1,), (1,)), ((), ()))

    partial_keys(0)
    pl.semaphore_wait(barrier, 14 - yl + jnp.where(r > 0, NROW, 0) - jnp.where(is_mid, 1, 0))
    k_scatter.start(0)
    for g in range(1, GROUPS):
        partial_keys(g)
        k_scatter.start(g)

    slab_copy.wait()

    @pl.when(low)
    def _():
        add_rows(slab_send, 0, far_rows, [(slab_f, 0)])
        slab_far().start()

    for i in range(2):
        cov_ready(i)
    for g in groups:
        k_scatter.middle(g)
    for i in range(2, 4):
        cov_ready(i)

    for g in groups:
        k_scatter.end(g, own, [], [])
        for h in range(2):
            add_rows(held.at[0, g, h], 0, ch, [(own, chunk_at(g, h, r))])
            relay_copy(g, h, 0).start()

        @pl.when(u > 0)
        def _(g=g):
            for h in range(2):
                relay_copy(g, h, 1).start()

        k_gather.start(g)
        lag_send(g, 0, 1, PLANE - u)

    for g in groups:
        lag_relayed(g)
    for g in groups:
        k_gather.middle(g)
    for g in groups:
        lag_pass(g)

    for i in range(4, tiles):
        cov_ready(i)

    @pl.when(jnp.logical_not(low))
    def _():
        slab_pad[...] = jnp.zeros_like(slab_pad)
        add_rows(slab_pad, tile + at_1 - start_1, far_rows, [(slab_f, 0)])
        slab_far().wait_recv()
        add_rows(slab_pad, at_0 - start_0, far_rows, [(slab_in, 0)])

    for g in groups:
        k_gather.end(g)

        @pl.when(low)
        def _(g=g):
            for h in range(2):
                win_far(g, h).start()

        @pl.when(r > 0)
        def _(g=g):
            def mirror(n):
                block = pl.ds(pl.multiple_of(n * tile, tile), tile)
                mir[rows_of(g), block] = lax.dot_general(
                    own[rows_of(g), :], cov[block, :], contract_last, preferred_element_type=F32
                ).astype(BF16)

            each(0, tiles, mirror)

            for h in range(2):
                others(0, NROW, lambda e, h=h: mir_copy(g, h, e, r - 1).start())

        @pl.when(is_mid)
        def _(g=g):
            for h in range(2):
                mir_stay(g, h).start()

        @pl.when(jnp.logical_not(low))
        def _(g=g):
            def narrow(n):
                block = pl.ds(pl.multiple_of(n * tile, tile), tile)
                nout_send[rows_of(g), block] = lax.dot_general(
                    own[rows_of(g), :], slab_pad[block, :], contract_last, preferred_element_type=F32
                ).astype(BF16)

            each(0, 2, narrow)
            nout_far(g).start()

    for g in groups:
        own_to_lag = pltpu.make_async_copy(own.at[rows_of(g)], lag.at[rows_of(g)], loc_sem)

        @pl.when(r == 0)
        def _(own_to_lag=own_to_lag):
            own_to_lag.start()
            own_to_lag.wait()

        @pl.when(r > 0)
        def _(g=g):
            for h in range(2):
                lag_got(g, h, 0)
            add_rows(lag, pl.multiple_of(g * group + x * (2 * ch), 2 * ch), 2 * ch, [(mid.at[0, g, 0], 0)])
            for y in range(2):
                add_rows(lag, chunk_at(g, 1, y * NX + x), ch, [(mid.at[0, g, 1], y * ch)])
            for d in range(1, NX):
                for part_at in range(3):
                    lag_second(g, d, part_at, behind(d)).wait_recv()

        @pl.when(low)
        def _(g=g):
            def step(n):
                block = pl.ds(pl.multiple_of(n * tile, tile), tile)
                direct[rows_of(g), block] = jnp.dot(
                    lag[rows_of(g), :], cov[:, block], preferred_element_type=F32
                ).astype(BF16)

            each(0, tiles, step)
            nout_far(g).wait_recv()

            def add_narrow(i):
                rows = pl.ds(pl.multiple_of(g * group + i * 64, 64), 64)
                for h, start in ((0, start_0), (1, start_1)):
                    columns = pl.ds(start, tile)
                    direct[rows, columns] = (
                        direct[rows, columns].astype(F32)
                        + nout[rows, pl.ds(h * tile, tile)].astype(F32)
                    ).astype(BF16)

            each(0, group // 64, add_narrow)

        @pl.when(jnp.logical_not(low))
        def _(g=g):
            for h in range(2):
                win_far(g, h).wait_recv()

            def step(n):
                block = pl.ds(pl.multiple_of(n * tile, tile), tile)
                direct[rows_of(g), block] = (
                    jnp.dot(lag[rows_of(g), :], cov[:, block], preferred_element_type=F32)
                    + jnp.dot(win[rows_of(g), :], slab_pad[:, block], preferred_element_type=F32)
                ).astype(BF16)

            each(0, tiles, step)

        q_scatter.start(g)

    for g in groups:
        def got_mir(i, g=g):
            for h in range(2):
                mir_copy(g, h, r, i - 1).wait_recv()

        others(1, NROW, got_mir)

        @pl.when(is_mid)
        def _(g=g):
            for h in range(2):
                mir_stay(g, h).wait()

        add_slots(crossed.at[0, g], g, PLANE - u - 1, 2 * PLANE - u - 1)
        cross_copy(g, 0).start()

        @pl.when(u > 0)
        def _(g=g):
            add_slots(crossed.at[1, g], g, 2 * PLANE - u - 1, NROW - 1)
            cross_copy(g, 1).start()

        add_slots(q_sum.at[g], g, 0, PLANE - u - 1)
    for g in groups:
        q_scatter.middle(g)

    for g in groups:
        cross_copy(g, 0).wait_recv()
        total = q_sum.at[g]
        add_rows(total, 0, 2 * ch, [(total, 0), (cross_in.at[0, g], 0)])

        @pl.when(u > 0)
        def _(g=g, total=total):
            cross_copy(g, 1).wait_recv()
            add_rows(total, 0, 2 * ch, [(total, 0), (cross_in.at[1, g], 0)])

        q_scatter.end(g, q_all, [(total, 0)], [(total, ch)])
        q_gather.start(g)

    def result(g):
        return pltpu.make_async_copy(q_all.at[rows_of(g)], out_ref.at[rows_of(g)], out_sem.at[g])

    for g in groups:
        q_gather.middle(g)
    for g in groups:
        q_gather.end(g)
        result(g).start()

    for g in groups:
        k_scatter.sent(g)
        q_scatter.sent(g)
        k_gather.sent(g)
        q_gather.sent(g)

        lag_sent(g)

        @pl.when(r > 0)
        def _(g=g):
            def mir_sent(e):
                for h in range(2):
                    mir_copy(g, h, e, r - 1).wait_send()

            others(0, NROW, mir_sent)

        cross_copy(g, 0).wait_send()

        @pl.when(u > 0)
        def _(g=g):
            cross_copy(g, 1).wait_send()

        @pl.when(low)
        def _(g=g):
            for h in range(2):
                win_far(g, h).wait_send()

        @pl.when(jnp.logical_not(low))
        def _(g=g):
            nout_far(g).wait_send()

    @pl.when(low)
    def _():
        slab_far().wait_send()

    for g in groups:
        result(g).wait()


def delta_kernel(residual_ref, q_ref, out_ref):
    out_ref[...] = jnp.dot(residual_ref[...], q_ref[...], preferred_element_type=F32).astype(
        out_ref.dtype
    )


def shards(tokens, edit_src, cov_tiles, cov_far, residual):
    edits, context = edit_src.shape
    tok_dev, width = tokens.shape
    ch = edits // GROUPS // 2 // NROW
    far_rows = cov_far.shape[1]
    tiles = width // 256

    def buf(*shape, dtype=BF16):
        return pltpu.VMEM(shape, dtype)

    def dma(*shape):
        return pltpu.SemaphoreType.DMA(shape)

    def reduce_bufs():
        return [
            buf(GROUPS, NX - 1, 2 * ch, width), buf(GROUPS, ch, width), buf(GROUPS, NX * ch, width),
            buf(GROUPS, NX - 1, ch, width), buf(GROUPS, 2 * ch, width), buf(GROUPS, NX * ch, width),
        ]

    q_block = pl.pallas_call(
        kernel,
        name="edit_product",
        out_shape=jax.ShapeDtypeStruct((edits, width), BF16),
        in_specs=[
            pl.BlockSpec(memory_space=pltpu.VMEM),
            pl.BlockSpec(memory_space=pltpu.VMEM),
            pl.BlockSpec(memory_space=pl.ANY),
            pl.BlockSpec(memory_space=pl.ANY),
        ],
        out_specs=pl.BlockSpec(memory_space=pl.ANY),
        scratch_shapes=[
            buf(edits, tok_dev), buf(edits, width),
            buf(width, width, dtype=F32), buf(width, width),
            buf(far_rows, width, dtype=F32), buf(far_rows, width), buf(far_rows, width), buf(512, width),
            buf(edits, width), buf(edits, width), buf(edits, width), buf(edits, width),
            buf(edits, 512), buf(edits, 512), buf(edits, 512),
            *reduce_bufs(),
            *reduce_bufs(),
            buf(NROW - 1, GROUPS, 2, ch, width), buf(GROUPS, 2 * ch, width, dtype=F32), buf(edits, width),
            buf(3, GROUPS, 2, ch, width), buf(NX, GROUPS, 2, 2 * ch, width), buf(2, GROUPS, 2 * ch, width), buf(2, GROUPS, 2 * ch, width),
            dma(tiles), pltpu.SemaphoreType.DMA, pltpu.SemaphoreType.DMA, dma(GROUPS),
            *[dma(GROUPS, 8) for _ in range(8)],
            dma(NROW, GROUPS, 2), dma(NX, 2, GROUPS, 2), dma(NX - 1, GROUPS, 3), dma(NX - 1, GROUPS, 3),
            dma(NROW, GROUPS, 2), dma(NROW - 1, GROUPS, 2),
            pltpu.SemaphoreType.DMA, pltpu.SemaphoreType.DMA,
            dma(GROUPS, 2), dma(GROUPS, 2), dma(GROUPS), dma(GROUPS),
            dma(2, GROUPS, 2), dma(2, GROUPS, 2), dma(2, GROUPS), dma(2, GROUPS), dma(GROUPS, 2), dma(GROUPS, 2),
        ],
        compiler_params=pltpu.CompilerParams(
            collective_id=0, has_side_effects=True, vmem_limit_bytes=60 * 2**20
        ),
    )(edit_src.T, tokens, cov_tiles, cov_far)

    rows = residual.shape[0]
    step = 256
    return pl.pallas_call(
        delta_kernel,
        name="delta",
        grid=(rows // step,),
        out_shape=jax.ShapeDtypeStruct((rows, width), BF16),
        in_specs=[
            pl.BlockSpec((step, edits), lambda i: (i, 0)),
            pl.BlockSpec((edits, width), lambda i: (0, 0)),
        ],
        out_specs=pl.BlockSpec((step, width), lambda i: (i, 0)),
        compiler_params=pltpu.CompilerParams(vmem_limit_bytes=32 * 2**20),
    )(residual, q_block)


def solution(mesh):
    placed = (
        P("row", "col"),
        P(),
        P("row", "col", None, None),
        P("col", "row", None),
        P("row", None),
    )
    return jax.shard_map(
        shards, mesh=mesh, in_specs=placed, out_specs=P("row", "col"), check_vma=False
    )
```

```python
import functools

import jax
import jax.numpy as jnp
from jax import lax
from jax.experimental import pallas as pl
from jax.experimental.pallas import tpu as pltpu
from jax.sharding import PartitionSpec as P

MESH = pl.DeviceIdType.MESH
F32 = jnp.float32
BF16 = jnp.bfloat16
NX = 4
NROW = 8
NCOL = 16
PLANE = 4
GROUPS = 2
SLAB = 16


def remote(src, dst, send_sem, recv_sem, row, col):
    return pltpu.make_async_remote_copy(
        src_ref=src,
        dst_ref=dst,
        send_sem=send_sem,
        recv_sem=recv_sem,
        device_id=(row, col),
        device_id_type=MESH,
    )


def add_rows(out_ref, out_at, rows, terms):
    def step(i, carry):
        at = pl.multiple_of(i * SLAB, SLAB)
        total = None
        for ref, start in terms:
            part = ref[pl.ds(pl.multiple_of(start + at, SLAB), SLAB), :].astype(F32)
            total = part if total is None else total + part
        out_ref[pl.ds(pl.multiple_of(out_at + at, SLAB), SLAB), :] = total.astype(out_ref.dtype)
        return carry

    lax.fori_loop(0, rows // SLAB, step, 0)


def kernel(
    edit_ref, tok_ref, cov_ref, far_ref, out_ref,
    counts, part, cov_f, cov, slab_f, slab_send, slab_in, slab_pad,
    own, lag, mir, direct, win, nout_send, nout,
    k_ra1, k_ra2, k_rb1, k_rb2, k_sa, k_sb, k_pass, k_sum,
    q_ra1, q_ra2, q_rb1, q_rb2, q_sa, q_sb, q_pass, q_part, m_in, q_sum, q_all, held, mid, crossed, cross_in,
    cov_sem, slab_sem, loc_sem, out_sem,
    krs_s, krs_r, kag_s, kag_r, qrs_s, qrs_r, qag_s, qag_r,
    first_s, first_r, second_s, second_r, mir_s, mir_r, slab_s, slab_r, win_s, win_r, nout_s, nout_r,
    rel_s, rel_r, cross_s, cross_r, stay_sem, keep_sem,
):
    r = lax.axis_index("row")
    c = lax.axis_index("col")
    x = r % NX
    yl = r // NX
    ry = (r + NX) % NROW
    edits, width = own.shape
    group = edits // GROUPS
    half = group // 2
    ch = half // NROW
    tok_dev = tok_ref.shape[0]
    tile = 256
    tiles = width // tile
    far_rows = slab_f.shape[0]
    groups = range(GROUPS)

    def across(d):
        return yl * NX + (x + d) % NX

    def behind(d):
        return (x + NX - d) % NX

    u = c % PLANE
    plane = c - u
    is_mid = r == PLANE

    def ahead(i):
        return plane + (u + i) % PLANE

    source_col = plane + (u + NCOL - r) % PLANE
    up_col = (c + PLANE) % NCOL
    down_col = (c + NCOL - PLANE) % NCOL
    low = c < NCOL // 2
    far_col = (c + NCOL // 2) % NCOL

    def chunk_at(g, h, row):
        if h == 0:
            at = (row % NX) * (2 * ch) + (row // NX) * ch
        else:
            at = half + (row // NX) * (NX * ch) + (row % NX) * ch
        return pl.multiple_of(g * group + at, ch)

    def chunk(g, h, row):
        return pl.ds(chunk_at(g, h, row), ch)

    def each(low_end, high_end, do):
        def step(i, carry):
            do(i)
            return carry

        lax.fori_loop(low_end, high_end, step, 0)

    def others(low_end, high_end, do):
        def step(i):
            @pl.when(jnp.logical_not(jnp.logical_and(is_mid, i == PLANE)))
            def _():
                do(i)

        each(low_end, high_end, step)

    barrier = pltpu.get_barrier_semaphore()

    def greet(row, col):
        pl.semaphore_signal(barrier, inc=1, device_id=(row, col), device_id_type=MESH)

    for d in range(1, NX):
        greet(across(d), c)
    greet(ry, c)
    greet(r, far_col)
    greet(r, up_col)
    greet(r, down_col)
    others(1, NROW, lambda i: greet(i, ahead(i)))
    for d in range(NX):
        lag_by = yl * NX + (x + d) % NX

        @pl.when(lag_by > 0)
        def _(lag_by=lag_by):
            greet(x, plane + (u + NROW - lag_by) % PLANE)

            @pl.when(lag_by != PLANE)
            def _():
                greet(NX + x, plane + (u + NROW - lag_by) % PLANE)

    def cov_copy(i):
        rows = pl.ds(i * tile, tile)
        return pltpu.make_async_copy(cov_ref.at[0, 0, rows], cov_f.at[rows], cov_sem.at[i])

    def cov_ready(i):
        cov_copy(i).wait()
        add_rows(cov, i * tile, tile, [(cov_f, i * tile)])

    slab_copy = pltpu.make_async_copy(far_ref.at[0], slab_f, slab_sem)
    slab_copy.start()
    for i in range(tiles):
        cov_copy(i).start()

    def partial_keys(g):
        for at in range(g * group, (g + 1) * group, 128):
            relative = edit_ref[:, at : at + 128] - r * tok_dev
            slots = lax.broadcasted_iota(jnp.int32, (tok_dev, 128), 0)
            total = jnp.zeros((tok_dev, 128), F32)
            for j in range(edit_ref.shape[0]):
                total = total + (relative[j : j + 1, :] == slots).astype(F32)
            counts[at : at + 128, :] = (total / edit_ref.shape[0]).T.astype(BF16)

        def step(n):
            columns = pl.ds(pl.multiple_of(n * tile, tile), tile)
            part[pl.ds(g * group, group), columns] = jnp.dot(
                counts[pl.ds(g * group, group), :], tok_ref[:, columns], preferred_element_type=F32
            ).astype(BF16)

        each(0, tiles, step)

    class Scatter:
        def __init__(self, src, ra1, ra2, rb1, rb2, sa, sb, passed, summed, ss, rs):
            self.src, self.ra1, self.ra2, self.rb1, self.rb2 = src, ra1, ra2, rb1, rb2
            self.sa, self.sb, self.passed, self.summed, self.ss, self.rs = sa, sb, passed, summed, ss, rs

        def half_at(self, g, d, part_at):
            return pl.multiple_of(g * group + ((x + d) % NX) * (2 * ch) + part_at * ch, ch)

        def a1(self, g, way, whole):
            d = 1 if way == 0 else 3
            if whole:
                src, dst = self.half_at(g, d, 1 - way), self.ra1.at[g, way, pl.ds((1 - way) * ch, ch)]
            else:
                src, dst = self.half_at(g, 2, way), self.passed.at[g, way]
            sem = 2 * way + (1 if whole else 0)
            return remote(
                self.src.at[pl.ds(src, ch)], dst, self.ss.at[g, sem], self.rs.at[g, sem], across(d), c
            )

        def a1_on(self, g, way):
            return remote(
                self.summed.at[g, way], self.ra1.at[g, way, pl.ds(way * ch, ch)],
                self.ss.at[g, 8 + way], self.rs.at[g, 8 + way], across(1 if way == 0 else 3), c,
            )

        def b1(self, g):
            rows = pl.ds(pl.multiple_of(g * group + half + (1 - yl) * (NX * ch), NX * ch), NX * ch)
            return remote(self.src.at[rows], self.rb1.at[g], self.ss.at[g, 10], self.rs.at[g, 10], ry, c)

        def a2(self, g):
            rows = pl.ds(pl.multiple_of((1 - yl) * ch, ch), ch)
            return remote(self.sa.at[g, rows], self.ra2.at[g], self.ss.at[g, 4], self.rs.at[g, 4], ry, c)

        def b2(self, g, d):
            rows = pl.ds(pl.multiple_of(((x + d) % NX) * ch, ch), ch)
            return remote(
                self.sb.at[g, rows], self.rb2.at[g, d - 1], self.ss.at[g, 4 + d], self.rs.at[g, 4 + d], across(d), c
            )

        def start(self, g):
            self.b1(g).start()
            for whole in (False, True):
                for way in range(2):
                    self.a1(g, way, whole).start()

        def middle(self, g):
            for way in range(2):
                self.a1(g, way, False).wait_recv()
                at = self.half_at(g, 1 if way == 0 else 3, way)
                add_rows(self.summed.at[g, way], 0, ch, [(self.src, at), (self.passed.at[g, way], 0)])
                self.a1_on(g, way).start()
            self.b1(g).wait_recv()
            add_rows(
                self.sb.at[g], 0, NX * ch, [(self.src, g * group + half + yl * (NX * ch)), (self.rb1.at[g], 0)]
            )
            for d in (1, 3, 2):
                self.b2(g, d).start()

        def turn(self, g):
            for way in range(2):
                self.a1(g, way, True).wait_recv()
                self.a1_on(g, way).wait_recv()
            add_rows(
                self.sa.at[g], 0, 2 * ch,
                [(self.src, g * group + x * (2 * ch))] + [(self.ra1.at[g, way], 0) for way in range(2)],
            )
            self.a2(g).start()

        def end(self, g, out, a_more, b_more):
            self.a2(g).wait_recv()
            add_rows(out, chunk_at(g, 0, r), ch, [(self.sa.at[g], yl * ch), (self.ra2.at[g], 0)] + a_more)
            for d in range(1, NX):
                self.b2(g, d).wait_recv()
            add_rows(
                out, chunk_at(g, 1, r), ch,
                [(self.sb.at[g], x * ch)] + [(self.rb2.at[g, d], 0) for d in range(NX - 1)] + b_more,
            )

        def sent(self, g):
            self.b1(g).wait_send()
            self.a2(g).wait_send()
            for way in range(2):
                self.a1(g, way, False).wait_send()
                self.a1(g, way, True).wait_send()
                self.a1_on(g, way).wait_send()
            for d in range(1, NX):
                self.b2(g, d).wait_send()

    class Gather:
        def __init__(self, full, ss, rs):
            self.full, self.ss, self.rs = full, ss, rs

        def move(self, g, rows, sem, row):
            return remote(
                self.full.at[rows], self.full.at[rows], self.ss.at[g, sem], self.rs.at[g, sem], row, c
            )

        def a1(self, g, row):
            return self.move(g, chunk(g, 0, row), 0, ry)

        def b1(self, g, row, d):
            return self.move(g, chunk(g, 1, row), d, across(d))

        def a2(self, g, xx, d):
            rows = pl.ds(pl.multiple_of(g * group + xx * (2 * ch), 2 * ch), 2 * ch)
            return self.move(g, rows, 3 + d, across(d))

        def a2_on(self, g, xx, way):
            rows = pl.ds(pl.multiple_of(g * group + xx * (2 * ch) + way * ch, ch), ch)
            return self.move(g, rows, 8 + way, across(1 if way == 0 else 3))

        def turn(self, g):
            for way, d in ((0, 1), (1, 3)):
                self.a2(g, behind(d), d).wait_recv()
                self.a2_on(g, behind(d), way).start()

        def b2(self, g, yy):
            rows = pl.ds(pl.multiple_of(g * group + half + yy * (NX * ch), NX * ch), NX * ch)
            return self.move(g, rows, 7, ry)

        def start(self, g):
            self.a1(g, r).start()
            for d in (1, 3, 2):
                self.b1(g, r, d).start()

        def middle(self, g):
            self.a1(g, ry).wait_recv()
            for d in (1, 3):
                self.a2(g, x, d).start()
            for d in range(1, NX):
                self.b1(g, yl * NX + behind(d), d).wait_recv()
            self.b2(g, yl).start()

        def end(self, g):
            for way in range(2):
                self.a2_on(g, (x + 2) % NX, way).wait_recv()
            self.b2(g, 1 - yl).wait_recv()

        def sent(self, g):
            self.a1(g, r).wait_send()
            for d in range(1, NX):
                self.b1(g, r, d).wait_send()
            for way, d in ((0, 1), (1, 3)):
                self.a2(g, x, d).wait_send()
                self.a2_on(g, behind(d), way).wait_send()
            self.b2(g, yl).wait_send()

    def relay_copy(g, h, far):
        return remote(
            held.at[0, g, h], held.at[1 + far, g, h], rel_s.at[far, g, h], rel_r.at[far, g, h], r,
            far_col if far else up_col,
        )

    def lag_first(g, h, by, source, from_y):
        y, d = by // NX, (by % NX + NX - x) % NX
        place = mid.at[d, g, h, pl.ds(pl.multiple_of(from_y * ch, ch), ch)]
        return remote(
            source, place, first_s.at[by, g, h], first_r.at[d, from_y, g, h], y * NX + x, ahead(by)
        )

    def lag_stay(g, h):
        return pltpu.make_async_copy(
            held.at[1, g, h], mid.at[(NX - x) % NX, g, h, pl.ds(ch, ch)], keep_sem.at[g, h]
        )

    def here(by):
        return jnp.logical_and(yl == 1, by == PLANE)

    def lag_send(g, level, first, last):
        def send(by):
            @pl.when(jnp.logical_not(here(by)))
            def _():
                for h in range(2):
                    lag_first(g, h, by, held.at[level, g, h], yl).start()

        each(first, last, send)

    def lag_relayed(g):
        for h in range(2):
            relay_copy(g, h, 0).wait_recv()
        lag_send(g, 1, PLANE - u, 2 * PLANE - u)

        @pl.when(yl == 1)
        def _():
            for h in range(2):
                lag_stay(g, h).start()

        @pl.when(u > 0)
        def _():
            for h in range(2):
                relay_copy(g, h, 1).wait_recv()
            lag_send(g, 2, 2 * PLANE - u, NROW)

    def lag_got(g, h, d):
        by = across(d)
        lag_first(g, h, by, held.at[0, g, h], 0).wait_recv()

        @pl.when(here(by))
        def _():
            lag_stay(g, h).wait()

        @pl.when(jnp.logical_not(here(by)))
        def _():
            lag_first(g, h, by, held.at[0, g, h], 1).wait_recv()

    def lag_second(g, d, part_at, xx):
        if part_at == 0:
            source = mid.at[d, g, 0]
            rows = pl.ds(pl.multiple_of(g * group + xx * (2 * ch), 2 * ch), 2 * ch)
        else:
            source = mid.at[d, g, 1, pl.ds((part_at - 1) * ch, ch)]
            rows = chunk(g, 1, (part_at - 1) * NX + xx)
        return remote(
            source, lag.at[rows], second_s.at[d - 1, g, part_at], second_r.at[d - 1, g, part_at], across(d), c
        )

    def passing(d, do):
        @pl.when(across(d) > 0)
        def _():
            do(d)

    def lag_pass(g):
        def on(d):
            for h in range(2):
                lag_got(g, h, d)
                for part_at in (0,) if h == 0 else (1, 2):
                    lag_second(g, d, part_at, x).start()

        for d in (1, 3, 2):
            passing(d, on)

    def lag_sent(g):
        def first_sent(by):
            @pl.when(jnp.logical_not(here(by)))
            def _():
                for h in range(2):
                    lag_first(g, h, by, held.at[0, g, h], yl).wait_send()

        each(1, NROW, first_sent)
        for h in range(2):
            relay_copy(g, h, 0).wait_send()

        @pl.when(u > 0)
        def _():
            for h in range(2):
                relay_copy(g, h, 1).wait_send()

        def on(d):
            for part_at in range(3):
                lag_second(g, d, part_at, x).wait_send()

        for d in range(1, NX):
            passing(d, on)

    def mir_copy(g, h, e, slot):
        return remote(
            mir.at[chunk(g, h, e)], m_in.at[slot, g, h], mir_s.at[e, g, h], mir_r.at[slot, g, h], e, source_col
        )

    def mir_stay(g, h):
        return pltpu.make_async_copy(mir.at[chunk(g, h, r)], m_in.at[PLANE - 1, g, h], stay_sem.at[g, h])

    def cross_copy(g, far):
        return remote(
            crossed.at[far, g], cross_in.at[far, g], cross_s.at[far, g], cross_r.at[far, g], r,
            far_col if far else down_col,
        )

    def add_slots(out, g, first, last):
        for h in range(2):
            for at in range(0, ch, SLAB):
                rows = pl.ds(at, SLAB)
                total = lax.fori_loop(
                    first, last,
                    lambda slot, so_far: so_far + m_in[slot, g, h, rows, :].astype(F32),
                    jnp.zeros((SLAB, width), F32),
                )
                out[pl.ds(h * ch + at, SLAB), :] = total.astype(out.dtype)

    at_0 = r * far_rows
    at_1 = width // 2 + r * far_rows
    start_0 = pl.multiple_of(at_0 // 128 * 128, 128)
    start_1 = pl.multiple_of(jnp.minimum(at_1 // 128 * 128, width - tile), 128)

    def rows_of(g):
        return pl.ds(g * group, group)

    def slab_far():
        return remote(slab_send, slab_in, slab_s, slab_r, r, far_col)

    def win_far(g, h):
        columns = pl.ds(start_0 if h == 0 else start_1, tile)
        return remote(
            own.at[rows_of(g), columns], win.at[rows_of(g), pl.ds(h * tile, tile)],
            win_s.at[g, h], win_r.at[g, h], r, far_col,
        )

    def nout_far(g):
        return remote(nout_send.at[rows_of(g)], nout.at[rows_of(g)], nout_s.at[g], nout_r.at[g], r, far_col)

    k_scatter = Scatter(part, k_ra1, k_ra2, k_rb1, k_rb2, k_sa, k_sb, k_pass, k_sum, krs_s, krs_r)
    q_scatter = Scatter(direct, q_ra1, q_ra2, q_rb1, q_rb2, q_sa, q_sb, q_pass, q_part, qrs_s, qrs_r)
    k_gather = Gather(own, kag_s, kag_r)
    q_gather = Gather(q_all, qag_s, qag_r)
    contract_last = (((1,), (1,)), ((), ()))

    partial_keys(0)
    pl.semaphore_wait(barrier, 14 - yl + jnp.where(r > 0, NROW, 0) - jnp.where(is_mid, 1, 0))
    k_scatter.start(0)
    for g in range(1, GROUPS):
        partial_keys(g)
        k_scatter.start(g)

    slab_copy.wait()

    @pl.when(low)
    def _():
        add_rows(slab_send, 0, far_rows, [(slab_f, 0)])
        slab_far().start()

    for i in range(2):
        cov_ready(i)
    for g in groups:
        k_scatter.middle(g)
    for g in groups:
        k_scatter.turn(g)
    for i in range(2, 4):
        cov_ready(i)

    for g in groups:
        k_scatter.end(g, own, [], [])
        for h in range(2):
            add_rows(held.at[0, g, h], 0, ch, [(own, chunk_at(g, h, r))])
            relay_copy(g, h, 0).start()

        @pl.when(u > 0)
        def _(g=g):
            for h in range(2):
                relay_copy(g, h, 1).start()

        k_gather.start(g)
        lag_send(g, 0, 1, PLANE - u)

    for g in groups:
        lag_relayed(g)
    for g in groups:
        k_gather.middle(g)
    for g in groups:
        k_gather.turn(g)
    for g in groups:
        lag_pass(g)

    for i in range(4, tiles):
        cov_ready(i)

    @pl.when(jnp.logical_not(low))
    def _():
        slab_pad[...] = jnp.zeros_like(slab_pad)
        add_rows(slab_pad, tile + at_1 - start_1, far_rows, [(slab_f, 0)])
        slab_far().wait_recv()
        add_rows(slab_pad, at_0 - start_0, far_rows, [(slab_in, 0)])

    for g in groups:
        k_gather.end(g)

        @pl.when(low)
        def _(g=g):
            for h in range(2):
                win_far(g, h).start()

        @pl.when(r > 0)
        def _(g=g):
            def mirror(n):
                block = pl.ds(pl.multiple_of(n * tile, tile), tile)
                mir[rows_of(g), block] = lax.dot_general(
                    own[rows_of(g), :], cov[block, :], contract_last, preferred_element_type=F32
                ).astype(BF16)

            each(0, tiles, mirror)

            for h in range(2):
                others(0, NROW, lambda e, h=h: mir_copy(g, h, e, r - 1).start())

        @pl.when(is_mid)
        def _(g=g):
            for h in range(2):
                mir_stay(g, h).start()

        @pl.when(jnp.logical_not(low))
        def _(g=g):
            def narrow(n):
                block = pl.ds(pl.multiple_of(n * tile, tile), tile)
                nout_send[rows_of(g), block] = lax.dot_general(
                    own[rows_of(g), :], slab_pad[block, :], contract_last, preferred_element_type=F32
                ).astype(BF16)

            each(0, 2, narrow)
            nout_far(g).start()

    for g in groups:
        own_to_lag = pltpu.make_async_copy(own.at[rows_of(g)], lag.at[rows_of(g)], loc_sem)

        @pl.when(r == 0)
        def _(own_to_lag=own_to_lag):
            own_to_lag.start()
            own_to_lag.wait()

        @pl.when(r > 0)
        def _(g=g):
            for h in range(2):
                lag_got(g, h, 0)
            add_rows(lag, pl.multiple_of(g * group + x * (2 * ch), 2 * ch), 2 * ch, [(mid.at[0, g, 0], 0)])
            for y in range(2):
                add_rows(lag, chunk_at(g, 1, y * NX + x), ch, [(mid.at[0, g, 1], y * ch)])
            for d in range(1, NX):
                for part_at in range(3):
                    lag_second(g, d, part_at, behind(d)).wait_recv()

        @pl.when(low)
        def _(g=g):
            def step(n):
                block = pl.ds(pl.multiple_of(n * tile, tile), tile)
                direct[rows_of(g), block] = jnp.dot(
                    lag[rows_of(g), :], cov[:, block], preferred_element_type=F32
                ).astype(BF16)

            each(0, tiles, step)
            nout_far(g).wait_recv()

            def add_narrow(i):
                rows = pl.ds(pl.multiple_of(g * group + i * 64, 64), 64)
                for h, start in ((0, start_0), (1, start_1)):
                    columns = pl.ds(start, tile)
                    direct[rows, columns] = (
                        direct[rows, columns].astype(F32)
                        + nout[rows, pl.ds(h * tile, tile)].astype(F32)
                    ).astype(BF16)

            each(0, group // 64, add_narrow)

        @pl.when(jnp.logical_not(low))
        def _(g=g):
            for h in range(2):
                win_far(g, h).wait_recv()

            def step(n):
                block = pl.ds(pl.multiple_of(n * tile, tile), tile)
                direct[rows_of(g), block] = (
                    jnp.dot(lag[rows_of(g), :], cov[:, block], preferred_element_type=F32)
                    + jnp.dot(win[rows_of(g), :], slab_pad[:, block], preferred_element_type=F32)
                ).astype(BF16)

            each(0, tiles, step)

        q_scatter.start(g)

    for g in groups:
        def got_mir(i, g=g):
            for h in range(2):
                mir_copy(g, h, r, i - 1).wait_recv()

        others(1, NROW, got_mir)

        @pl.when(is_mid)
        def _(g=g):
            for h in range(2):
                mir_stay(g, h).wait()

        add_slots(crossed.at[0, g], g, PLANE - u - 1, 2 * PLANE - u - 1)
        cross_copy(g, 0).start()

        @pl.when(u > 0)
        def _(g=g):
            add_slots(crossed.at[1, g], g, 2 * PLANE - u - 1, NROW - 1)
            cross_copy(g, 1).start()

        add_slots(q_sum.at[g], g, 0, PLANE - u - 1)
    for g in groups:
        q_scatter.middle(g)
    for g in groups:
        q_scatter.turn(g)

    for g in groups:
        cross_copy(g, 0).wait_recv()
        total = q_sum.at[g]
        add_rows(total, 0, 2 * ch, [(total, 0), (cross_in.at[0, g], 0)])

        @pl.when(u > 0)
        def _(g=g, total=total):
            cross_copy(g, 1).wait_recv()
            add_rows(total, 0, 2 * ch, [(total, 0), (cross_in.at[1, g], 0)])

        q_scatter.end(g, q_all, [(total, 0)], [(total, ch)])
        q_gather.start(g)

    def result(g):
        return pltpu.make_async_copy(q_all.at[rows_of(g)], out_ref.at[rows_of(g)], out_sem.at[g])

    for g in groups:
        q_gather.middle(g)
    for g in groups:
        q_gather.turn(g)
    for g in groups:
        q_gather.end(g)
        result(g).start()

    for g in groups:
        k_scatter.sent(g)
        q_scatter.sent(g)
        k_gather.sent(g)
        q_gather.sent(g)

        lag_sent(g)

        @pl.when(r > 0)
        def _(g=g):
            def mir_sent(e):
                for h in range(2):
                    mir_copy(g, h, e, r - 1).wait_send()

            others(0, NROW, mir_sent)

        cross_copy(g, 0).wait_send()

        @pl.when(u > 0)
        def _(g=g):
            cross_copy(g, 1).wait_send()

        @pl.when(low)
        def _(g=g):
            for h in range(2):
                win_far(g, h).wait_send()

        @pl.when(jnp.logical_not(low))
        def _(g=g):
            nout_far(g).wait_send()

    @pl.when(low)
    def _():
        slab_far().wait_send()

    for g in groups:
        result(g).wait()


def delta_kernel(residual_ref, q_ref, out_ref):
    out_ref[...] = jnp.dot(residual_ref[...], q_ref[...], preferred_element_type=F32).astype(
        out_ref.dtype
    )


def shards(tokens, edit_src, cov_tiles, cov_far, residual):
    edits, context = edit_src.shape
    tok_dev, width = tokens.shape
    ch = edits // GROUPS // 2 // NROW
    far_rows = cov_far.shape[1]
    tiles = width // 256

    def buf(*shape, dtype=BF16):
        return pltpu.VMEM(shape, dtype)

    def dma(*shape):
        return pltpu.SemaphoreType.DMA(shape)

    def reduce_bufs():
        return [
            buf(GROUPS, 2, 2 * ch, width), buf(GROUPS, ch, width), buf(GROUPS, NX * ch, width),
            buf(GROUPS, NX - 1, ch, width), buf(GROUPS, 2 * ch, width), buf(GROUPS, NX * ch, width),
            buf(GROUPS, 2, ch, width), buf(GROUPS, 2, ch, width),
        ]

    q_block = pl.pallas_call(
        kernel,
        name="edit_product",
        out_shape=jax.ShapeDtypeStruct((edits, width), BF16),
        in_specs=[
            pl.BlockSpec(memory_space=pltpu.VMEM),
            pl.BlockSpec(memory_space=pltpu.VMEM),
            pl.BlockSpec(memory_space=pl.ANY),
            pl.BlockSpec(memory_space=pl.ANY),
        ],
        out_specs=pl.BlockSpec(memory_space=pl.ANY),
        scratch_shapes=[
            buf(edits, tok_dev), buf(edits, width),
            buf(width, width, dtype=F32), buf(width, width),
            buf(far_rows, width, dtype=F32), buf(far_rows, width), buf(far_rows, width), buf(512, width),
            buf(edits, width), buf(edits, width), buf(edits, width), buf(edits, width),
            buf(edits, 512), buf(edits, 512), buf(edits, 512),
            *reduce_bufs(),
            *reduce_bufs(),
            buf(NROW - 1, GROUPS, 2, ch, width), buf(GROUPS, 2 * ch, width, dtype=F32), buf(edits, width),
            buf(3, GROUPS, 2, ch, width), buf(NX, GROUPS, 2, 2 * ch, width), buf(2, GROUPS, 2 * ch, width), buf(2, GROUPS, 2 * ch, width),
            dma(tiles), pltpu.SemaphoreType.DMA, pltpu.SemaphoreType.DMA, dma(GROUPS),
            *[dma(GROUPS, 12) for _ in range(8)],
            dma(NROW, GROUPS, 2), dma(NX, 2, GROUPS, 2), dma(NX - 1, GROUPS, 3), dma(NX - 1, GROUPS, 3),
            dma(NROW, GROUPS, 2), dma(NROW - 1, GROUPS, 2),
            pltpu.SemaphoreType.DMA, pltpu.SemaphoreType.DMA,
            dma(GROUPS, 2), dma(GROUPS, 2), dma(GROUPS), dma(GROUPS),
            dma(2, GROUPS, 2), dma(2, GROUPS, 2), dma(2, GROUPS), dma(2, GROUPS), dma(GROUPS, 2), dma(GROUPS, 2),
        ],
        compiler_params=pltpu.CompilerParams(
            collective_id=0, has_side_effects=True, vmem_limit_bytes=60 * 2**20
        ),
    )(edit_src.T, tokens, cov_tiles, cov_far)

    rows = residual.shape[0]
    step = 256
    return pl.pallas_call(
        delta_kernel,
        name="delta",
        grid=(rows // step,),
        out_shape=jax.ShapeDtypeStruct((rows, width), BF16),
        in_specs=[
            pl.BlockSpec((step, edits), lambda i: (i, 0)),
            pl.BlockSpec((edits, width), lambda i: (0, 0)),
        ],
        out_specs=pl.BlockSpec((step, width), lambda i: (i, 0)),
        compiler_params=pltpu.CompilerParams(vmem_limit_bytes=32 * 2**20),
    )(residual, q_block)


def solution(mesh):
    placed = (
        P("row", "col"),
        P(),
        P("row", "col", None, None),
        P("col", "row", None),
        P("row", None),
    )
    return jax.shard_map(
        shards, mesh=mesh, in_specs=placed, out_specs=P("row", "col"), check_vma=False
    )
```
